32 devices in a mesh: depth: 8 (over z, x), lat: 4 (over y, core).
Axes of the slice: x: 2, y: 2, z: 4, core: 2. Of those that a mesh axis runs over, the one named last changes fastest.
Arguments:
- phase: float32 [256, 256, 128], P('depth', 'lat'), may hold values from 0 to 1
- temper: float32 [256, 256, 128], P('depth', 'lat'), may hold values from -3 to 3
- iface_count: int32 [8, 4], P('depth', 'lat'), may hold values from 1 to 32, as said below
Outputs:
- phase_next: float32 [256, 256, 128], P('depth', 'lat')
- heat_next: float32 [256, 256, 128], P('depth', 'lat')
- picture: float32 [4, 256, 512], P(None, 'lat', 'depth')
The draws below stay inside these ranges and needn't reach their ends.
Inputs may be any that keep to these rules, and one draw needn't show every extreme that they name: `iface_count`: per brick a count of 1 to 32; some brick has exactly 32 and another exactly 1.
All inputs are finite; a program needn't handle non-finite values.
Results may differ from the reference program's by a relative error of at most 0.0003.
Values sent between devices are 32-bit elements; how exact they have to be, the bound alone decides.
A program may use at most 64 MiB of HBM per device.

```python
import math
import jax
import jax.numpy as jnp
import numpy as np
from jax import lax

CX = 32
CY = 64
VIEWS = 4
SWEEPS = 3
NX = 256
NY = 256
NZ = 128
N_DEPTH = 8
N_LAT = 4


def draw_iface_count(key, part):
    first_key = jax.random.fold_in(key, 11)
    second_key = jax.random.fold_in(key, 12)
    place_key = jax.random.fold_in(key, 13)
    first_draw = jax.random.randint(first_key, (N_DEPTH * N_LAT,), 1, CX + 1)
    second_draw = jax.random.randint(second_key, (N_DEPTH * N_LAT,), 1, CX + 1)
    counts = jnp.minimum(first_draw, second_draw).astype(jnp.int32)
    position = jax.random.randint(place_key, (), 0, N_DEPTH * N_LAT)
    counts = counts.at[position].set(CX)
    counts = counts.at[(position + 1) % (N_DEPTH * N_LAT)].set(1)
    return counts.reshape(N_DEPTH, N_LAT).astype(jnp.int32)


def levels(own_key, dims, shards, least, high):
    def one(dim, shards_of):
        steps = jax.random.uniform(jax.random.fold_in(jax.random.fold_in(own_key, 6), dim), (shards_of,), jnp.float32, least / len(shards), high / len(shards))
        return jnp.repeat(jnp.exp(steps), dims[dim] // shards_of).reshape((-1,) + (1,) * (len(dims) - dim - 1))

    loudness = one(*shards[0])
    for cut in shards[1:]:
        loudness = loudness * one(*cut)
    return loudness


def bell_draw(stream_key, dims, deviation, bound, shards=(), held_as=jnp.bfloat16):
    result = deviation * jax.random.normal(stream_key, dims, jnp.float32)
    if shards:
        result = result * levels(stream_key, dims, shards, -0.22, 0.18)
    return jnp.clip(result, -bound, bound).astype(held_as)


def setup_inputs(seed: int = 0) -> dict:
    key_list = jax.random.split(jax.random.key(seed), 4)
    phase = jnp.clip(1.0 * jax.random.uniform(key_list[0], (NX, NY, NZ), jnp.float32) ** levels(key_list[0], (NX, NY, NZ), ((0, 8), (1, 4)), -0.2, 0.2), 0.0, 1.0)
    temper = bell_draw(key_list[1], (NX, NY, NZ), 0.5, 3.0, ((0, 8), (1, 4)), jnp.float32)
    iface_count = draw_iface_count(jax.random.fold_in(key_list[3], 71), 0)
    return {"phase": phase, "temper": temper, "iface_count": iface_count}


DIFFUSION = (0.5, 2.0)
TIME_STEP = 0.4
COUPLE = 0.6
LATENT = 0.5
SHEAR_Y = (1.6, -1.6, 0.8, -1.2)
SHEAR_Z = (0.9, -0.6, -0.9, 0.3)
CENTERS = (-0.8, 0.0, 0.8)


def thetas(sweep_total):
    chebyshev = []
    for f in range(2):
        highest = 1.0 + 12.0 * DIFFUSION[f]
        entries = [0.5 * (highest + 1.0) + 0.5 * (highest - 1.0) * math.cos((2 * j + 1) * math.pi / (2 * sweep_total)) for j in range(sweep_total)]
        chebyshev.append(entries)
    return np.array(chebyshev)


def stencil(padded):
    summed = padded[:, 2:, 1:-1, 1:-1] + padded[:, :-2, 1:-1, 1:-1]
    summed = summed + padded[:, 1:-1, 2:, 1:-1] + padded[:, 1:-1, :-2, 1:-1]
    summed = summed + padded[:, 1:-1, 1:-1, 2:] + padded[:, 1:-1, 1:-1, :-2]
    return summed


def sources(phase, temper):
    reaction = phase * (1.0 - phase) * (phase - 0.5 + COUPLE * temper)
    return jnp.stack([phase + TIME_STEP * reaction, temper + LATENT * TIME_STEP * reaction])


def relax(current, source, diffusion, step_size, padded):
    applied = current + diffusion * (6.0 * current - stencil(padded))
    return current + (source - applied) / step_size


def offsets(layers, shear):
    offset = shear * np.arange(layers) / layers
    whole_part = np.floor(offset)
    return whole_part.astype(np.int32), offset - whole_part


def footprint(padded, layer_mask, opacity_scale):
    layers = padded.shape[1]
    row_count = padded.shape[2] - 4
    col_count = padded.shape[3] - 2
    layer_ids = jnp.arange(layers).astype(jnp.int32)[:, None]
    pictures = []
    for v in range(len(SHEAR_Y)):
        base_y, frac_y = offsets(layers, SHEAR_Y[v])
        base_z, frac_z = offsets(layers, SHEAR_Z[v])
        row_ids = jnp.asarray(base_y).astype(jnp.int32)[:, None] + 2 + jnp.arange(row_count).astype(jnp.int32)[None, :]
        near_row = padded[:, layer_ids, row_ids, :]
        far_row = padded[:, layer_ids, row_ids + 1, :]
        frac_row = jnp.asarray(frac_y, jnp.float32)[None, :, None, None]
        blended = (1.0 - frac_row) * near_row + frac_row * far_row
        col_ids = jnp.asarray(base_z).astype(jnp.int32)[:, None] + 1 + jnp.arange(col_count).astype(jnp.int32)[None, :]
        col_ids = jnp.broadcast_to(col_ids[None, :, None, :], (2, layers, row_count, col_count))
        near_col = jnp.take_along_axis(blended, col_ids, axis=3)
        far_col = jnp.take_along_axis(blended, col_ids + 1, axis=3)
        frac_col = jnp.asarray(frac_z, jnp.float32)[None, :, None, None]
        sampled = (1.0 - frac_col) * near_col + frac_col * far_col
        thickness = opacity_scale * sampled[0] * sampled[0] * layer_mask[:, :, None]
        optical = jnp.cumsum(thickness, axis=0)
        weight = jnp.exp(-(optical - thickness)) * (1.0 - jnp.exp(-thickness))
        colours = []
        for centre in CENTERS:
            distance = sampled[1] - centre
            colours.append(jnp.sum(weight / (1.0 + distance * distance), axis=0))
        colours.append(jnp.exp(-optical[-1]))
        pictures.append(jnp.stack(colours))
    return jnp.concatenate(pictures, axis=2)


def over_blend(in_front, behind):
    return jnp.concatenate([in_front[:3] + in_front[3:] * behind[:3], in_front[3:] * behind[3:]], axis=0)


def reference(phase, temper, iface_count):
    current = jnp.stack([phase, temper])
    source = sources(phase, temper)
    chebyshev = thetas(SWEEPS)
    diffusion = jnp.asarray(np.array(DIFFUSION), jnp.float32).reshape(2, 1, 1, 1)
    for k in range(SWEEPS):
        padded = jnp.pad(current, ((0, 0), (1, 1), (1, 1), (1, 1)))
        step_size = jnp.asarray(chebyshev[:, k], jnp.float32).reshape(2, 1, 1, 1)
        current = relax(current, source, diffusion, step_size, padded)
    padded_all = jnp.pad(current, ((0, 0), (0, 0), (2, 2), (1, 1)))
    local_layers = jnp.arange(CX).astype(jnp.int32)

    def render_slab(composite, d):
        slab_cells = lax.dynamic_slice_in_dim(padded_all, (d * CX).astype(jnp.int32), CX, 1)
        row_counts = jnp.repeat(iface_count[d], CY)
        layer_mask = (local_layers[:, None] < row_counts[None, :]).astype(jnp.float32)
        picture = footprint(slab_cells, layer_mask, 4.0 / NX)
        return over_blend(composite, picture), None

    start = jnp.concatenate([jnp.zeros((3, NY, VIEWS * NZ), jnp.float32), jnp.ones((1, NY, VIEWS * NZ), jnp.float32)], axis=0)
    composite, unused = lax.scan(render_slab, start, jnp.arange(N_DEPTH).astype(jnp.int32))
    return current[0], current[1], composite
```

```python
import functools
import math

import jax
import jax.numpy as jnp
import numpy as np
from jax import lax
from jax.experimental import pallas as pl
from jax.experimental.pallas import tpu as pltpu
from jax.sharding import PartitionSpec as P

SWEEPS = 3

DIFFUSION = (0.5, 2.0)
TIME_STEP = 0.4
COUPLE = 0.6
LATENT = 0.5
SHEAR_Y = (1.6, -1.6, 0.8, -1.2)
SHEAR_Z = (0.9, -0.6, -0.9, 0.3)
CENTERS = (-0.8, 0.0, 0.8)
VIEWS = len(SHEAR_Y)
MESH = pl.DeviceIdType.MESH
TILE = 8
REACH = 4


def thetas(sweep_total):
    chebyshev = []
    for f in range(2):
        highest = 1.0 + 12.0 * DIFFUSION[f]
        entries = [
            0.5 * (highest + 1.0)
            + 0.5 * (highest - 1.0) * math.cos((2 * j + 1) * math.pi / (2 * sweep_total))
            for j in range(sweep_total)
        ]
        chebyshev.append(entries)
    return np.array(chebyshev)


def over(front, behind):
    return [front[c] + front[3] * behind[c] for c in range(3)] + [front[3] * behind[3]]


def segments(x_lo, x_hi, shear, layers):
    runs = []
    for x in range(x_lo, x_hi):
        whole = int(math.floor(abs(shear) * x / layers))
        if runs and runs[-1][2] == whole:
            runs[-1][1] = x + 1
        else:
            runs.append([x, x + 1, whole])
    return runs


def kernel(
    depth_size,
    lat_size,
    swap,
    phase_ref,
    temper_ref,
    count_ref,
    phase_out,
    heat_out,
    picture_ref,
    u0,
    u1,
    u2,
    u3,
    src,
    keep,
    sent,
    xrecv,
    merged,
    zrecv,
    in_sem,
    out_sem,
    xs_sem,
    xr_sem,
    ys_sem,
    yr_sem,
    cs_sem,
    cr_sem,
    ps_sem,
    pr_sem,
    zs_sem,
    zr_sem,
):
    layers, rows, cols = phase_ref.shape
    halo = SWEEPS
    d = lax.axis_index("depth")
    l = lax.axis_index("lat")
    has_prev, has_next = d > 0, d < depth_size - 1
    has_low, has_high = l > 0, l < lat_size - 1
    up, down = lax.rem(d + 1, depth_size), lax.rem(d + depth_size - 1, depth_size)
    right, left = lax.rem(l + 1, lat_size), lax.rem(l + lat_size - 1, lat_size)
    xbit = lax.rem(d, 2)
    myz = d // 2
    partner = d + 1 - 2 * xbit
    fields = (phase_ref, temper_ref)

    local = [
        pltpu.make_async_copy(
            fields[f], u0.at[f, pl.ds(halo, layers), pl.ds(TILE, rows), :], in_sem.at[f]
        )
        for f in range(2)
    ]
    for copy in local:
        copy.start()

    barrier = pltpu.get_barrier_semaphore()
    greet = ((has_prev, (down, l)), (has_next, (up, l)), (has_low, (d, left)), (has_high, (d, right)))
    for there, device in greet:

        @pl.when(there)
        def _():
            pl.semaphore_signal(barrier, inc=1, device_id=device, device_id_type=MESH)

    if swap:
        for z in range(VIEWS):

            @pl.when(myz != z)
            def _():
                pl.semaphore_signal(
                    barrier, inc=1, device_id=(2 * z + xbit, l), device_id_type=MESH
                )

    @pl.when(d == 0)
    def _():
        u0[:, :halo] = jnp.zeros((2, halo, rows + 2 * TILE, cols), jnp.float32)

    @pl.when(d == depth_size - 1)
    def _():
        u0[:, halo + layers :] = jnp.zeros((2, halo, rows + 2 * TILE, cols), jnp.float32)

    for edge, first in ((l == 0, 0), (l == lat_size - 1, TILE + rows)):

        @pl.when(edge)
        def _():
            def clear(x, carry):
                for f in range(2):
                    u0[f, x, pl.ds(first, TILE), :] = jnp.zeros((TILE, cols), jnp.float32)
                return carry

            lax.fori_loop(0, layers + 2 * halo, clear, 0)

    peers = sum(
        jnp.minimum(n, 1) for n in (d, depth_size - 1 - d, l, lat_size - 1 - l)
    )
    pl.semaphore_wait(barrier, peers + (VIEWS - 1 if swap else 0))

    lat_copies, edge_copies, mid_copies, corner_copies = [], [], [], []
    for way in range(2):
        row_from, row_to = ((rows - TILE, 0), (0, TILE + rows))[way]
        for f in range(2):
            copy = pltpu.make_async_remote_copy(
                src_ref=fields[f].at[:, pl.ds(row_from, TILE), :],
                dst_ref=u0.at[f, pl.ds(halo, layers), pl.ds(row_to, TILE), :],
                send_sem=ys_sem.at[way, f],
                recv_sem=yr_sem.at[way, f],
                device_id=(d, (right, left)[way]),
                device_id_type=MESH,
            )
            lat_copies.append(((has_high, has_low)[way], (has_low, has_high)[way], copy))
    pieces = ((0, TILE), (rows - TILE, TILE), (TILE, rows - 2 * TILE))
    for piece, (row, size) in enumerate(pieces):
        for way in range(2):
            layer_from, layer_to = ((layers - halo, 0), (0, halo + layers))[way]
            for f in range(2):
                copy = pltpu.make_async_remote_copy(
                    src_ref=fields[f].at[pl.ds(layer_from, halo), pl.ds(row, size), :],
                    dst_ref=u0.at[f, pl.ds(layer_to, halo), pl.ds(TILE + row, size), :],
                    send_sem=xs_sem.at[piece, way, f],
                    recv_sem=xr_sem.at[piece, way, f],
                    device_id=((up, down)[way], l),
                    device_id_type=MESH,
                )
                entry = ((has_next, has_prev)[way], (has_prev, has_next)[way], copy)
                (mid_copies if piece == 2 else edge_copies).append(entry)
    for side in range(2):
        layer = (0, halo + layers)[side]
        filled = (has_prev, has_next)[side]
        for way in range(2):
            row_from, row_to = ((rows, 0), (TILE, TILE + rows))[way]
            copy = pltpu.make_async_remote_copy(
                src_ref=u0.at[:, pl.ds(layer, halo), pl.ds(row_from, TILE), :],
                dst_ref=u0.at[:, pl.ds(layer, halo), pl.ds(row_to, TILE), :],
                send_sem=cs_sem.at[side, way],
                recv_sem=cr_sem.at[side, way],
                device_id=(d, (right, left)[way]),
                device_id_type=MESH,
            )
            sends = jnp.logical_and(filled, (has_high, has_low)[way])
            receives = jnp.logical_and(filled, (has_low, has_high)[way])
            corner_copies.append((sends, receives, copy))

    def start(entries):
        for sends, _receives, copy in entries:
            pl.when(sends)(copy.start)

    def arrive(entries):
        for _sends, receives, copy in entries:
            pl.when(receives)(copy.wait_recv)

    def leave(entries):
        for sends, _receives, copy in entries:
            pl.when(sends)(copy.wait_send)

    start(edge_copies)
    start(lat_copies)
    start(mid_copies)
    for copy in local:
        copy.wait()
    arrive(lat_copies)

    chebyshev = thetas(SWEEPS)
    first_row = TILE - REACH
    span = rows + 2 * REACH
    chunk = next(n for n in (24, 16, 8) if span % n == 0)
    lane = lax.broadcasted_iota(jnp.int32, (chunk, cols), 1)
    row_id = lax.broadcasted_iota(jnp.int32, (chunk, cols), 0)
    low_mask = jnp.where(jnp.logical_or(row_id >= REACH, has_low), 1.0, 0.0)
    high_mask = jnp.where(jnp.logical_or(row_id < chunk - REACH, has_high), 1.0, 0.0)

    def sweep(k, before, after, x_lo, x_hi, edge):
        def body(x, carry):
            if edge:
                inside = jnp.logical_and(
                    jnp.logical_or(x >= halo, has_prev),
                    jnp.logical_or(x < halo + layers, has_next),
                )
                factor = jnp.where(inside, 1.0, 0.0)
            for r0 in range(first_row, first_row + span, chunk):
                here = pl.ds(r0, chunk)
                values = [before[f, x, here, :] for f in range(2)]
                if k == 0:
                    p, t = values
                    reaction = p * (1.0 - p) * (p - 0.5 + COUPLE * t)
                    sources = [p + TIME_STEP * reaction, t + LATENT * TIME_STEP * reaction]
                    for f in range(2):
                        src[f, x, here, :] = sources[f]
                else:
                    sources = [src[f, x, here, :] for f in range(2)]
                for f in range(2):
                    u = values[f]
                    around = before[f, x - 1, here, :] + before[f, x + 1, here, :]
                    around = around + (
                        before[f, x, pl.ds(r0 - 1, chunk), :] + before[f, x, pl.ds(r0 + 1, chunk), :]
                    )
                    around = around + jnp.where(lane == 0, 0.0, pltpu.roll(u, 1, 1))
                    around = around + jnp.where(lane == cols - 1, 0.0, pltpu.roll(u, cols - 1, 1))
                    theta = chebyshev[f, k]
                    new = (
                        float(1.0 - (1.0 + 6.0 * DIFFUSION[f]) / theta) * u
                        + float(1.0 / theta) * sources[f]
                        + float(DIFFUSION[f] / theta) * around
                    )
                    if r0 == first_row:
                        new = new * low_mask
                    if r0 + chunk == first_row + span:
                        new = new * high_mask
                    if edge:
                        new = new * factor
                    after[f, x, here, :] = new
            return carry

        lax.fori_loop(x_lo, x_hi, body, 0)

    stages = (u0, u1, u2, u3)
    total = layers + 2 * halo
    for k in range(SWEEPS):
        sweep(k, stages[k], stages[k + 1], halo + 1 + k, halo + layers - 1 - k, False)

    arrive(edge_copies)
    start(corner_copies)
    arrive(mid_copies)
    arrive(corner_copies)
    for k in range(SWEEPS):
        sweep(k, stages[k], stages[k + 1], 1 + k, halo + 1 + k, True)
        sweep(k, stages[k], stages[k + 1], halo + layers - 1 - k, total - 1 - k, True)

    outs = [
        pltpu.make_async_copy(
            u3.at[f, pl.ds(halo, layers), pl.ds(TILE, rows), :],
            (phase_out, heat_out)[f],
            out_sem.at[f],
        )
        for f in range(2)
    ]
    for copy in outs:
        copy.start()

    half = rows // 2
    count = count_ref[0, 0]
    lane1 = lax.broadcasted_iota(jnp.int32, (1, cols), 1)
    opacity = 4.0 / (layers * depth_size)

    def render(v, r0, x_lo, x_hi, carry):
        sy = 1 if SHEAR_Y[v] > 0 else -1
        sz = 1 if SHEAR_Z[v] > 0 else -1
        inside = jnp.where(lane1 == (cols - 1 if sz > 0 else 0), 0.0, 1.0)
        for lo, hi, whole in segments(x_lo, x_hi, SHEAR_Y[v], layers):

            def body(x, carry):
                trans, red, green, blue = carry
                xf = x.astype(jnp.float32)
                fy = xf * (abs(SHEAR_Y[v]) / layers) - whole
                fz = xf * (abs(SHEAR_Z[v]) / layers)
                far_z = inside * fz
                sampled = []
                for f in range(2):
                    near = u3[f, x + halo, pl.ds(TILE + r0 + sy * whole, half), :]
                    far = u3[f, x + halo, pl.ds(TILE + r0 + sy * (whole + 1), half), :]
                    b = near + fy * (far - near)
                    beside = pltpu.roll(b, cols - 1 if sz > 0 else 1, 1)
                    sampled.append((1.0 - fz) * b + far_z * beside)
                scale = jnp.where(x < count, -opacity, 0.0)
                after = trans * jnp.exp(scale * sampled[0] * sampled[0])
                weight = trans - after
                s = sampled[1]
                q = s * s
                d1 = q + 1.0
                a = q + (1.0 + CENTERS[2] * CENTERS[2])
                b = (2.0 * CENTERS[2]) * s
                d0, d2 = a + b, a - b
                sides = d0 * d2
                wr = weight / (sides * d1)
                wd = wr * d1
                return (after, red + wd * d2, green + wr * sides, blue + wd * d0)

            carry = lax.fori_loop(lo, hi, body, carry)
        return carry

    zero = jnp.zeros((half, cols), jnp.float32)
    one = jnp.ones((half, cols), jnp.float32)

    def picture_of(v):
        parts = []
        for r0 in (0, half):
            trans, red, green, blue = render(v, r0, 0, layers, (one, zero, zero, zero))
            parts.append([red, green, blue, trans])
        return parts

    if not swap:
        for v in range(VIEWS):
            for h, part in enumerate(picture_of(v)):
                for c in range(4):
                    picture_ref[c, h * half : (h + 1) * half, v * cols : (v + 1) * cols] = part[c]
    else:
        left_lanes = lax.broadcasted_iota(jnp.int32, (half, cols), 1) < cols // 2
        pair_copies = [
            pltpu.make_async_remote_copy(
                src_ref=sent.at[v],
                dst_ref=xrecv.at[v],
                send_sem=ps_sem.at[v],
                recv_sem=pr_sem.at[v],
                device_id=(partner, l),
                device_id_type=MESH,
            )
            for v in range(VIEWS)
        ]
        group_copies = [
            pltpu.make_async_remote_copy(
                src_ref=merged.at[v],
                dst_ref=zrecv.at[myz],
                send_sem=zs_sem.at[v],
                recv_sem=zr_sem.at[myz],
                device_id=(2 * v + xbit, l),
                device_id_type=MESH,
            )
            for v in range(VIEWS)
        ]

        def send_pair(v):
            lo, hi = picture_of(v)
            for c in range(4):
                lower = jnp.where(left_lanes, lo[c], pltpu.roll(hi[c], cols // 2, 1))
                upper = jnp.where(left_lanes, pltpu.roll(lo[c], cols // 2, 1), hi[c])
                keep[v, c] = jnp.where(xbit == 0, lower, upper)
                sent[v, c] = jnp.where(xbit == 0, upper, lower)
            pair_copies[v].start()

        def send_group(v):
            pair_copies[v].wait_recv()
            mine = [keep[v, c] for c in range(4)]
            other = [xrecv[v, c] for c in range(4)]
            front = [jnp.where(xbit == 0, m, o) for m, o in zip(mine, other)]
            behind = [jnp.where(xbit == 0, o, m) for m, o in zip(mine, other)]
            result = over(front, behind)

            @pl.when(myz == v)
            def _():
                for c in range(4):
                    zrecv[v, c] = result[c]

            @pl.when(myz != v)
            def _():
                for c in range(4):
                    merged[v, c] = result[c]
                group_copies[v].start()

        order = [0, VIEWS - 1] + list(range(1, VIEWS - 1))
        for place, v in enumerate(order):
            send_pair(v)
            if place:
                send_group(order[place - 1])
        send_group(order[-1])

        for s in range(VIEWS):

            @pl.when(myz != s)
            def _():
                pltpu.make_async_remote_copy(
                    src_ref=merged.at[s],
                    dst_ref=zrecv.at[s],
                    send_sem=zs_sem.at[s],
                    recv_sem=zr_sem.at[s],
                    device_id=(2 * s + xbit, l),
                    device_id_type=MESH,
                ).wait_recv()

        result = [zrecv[VIEWS - 1, c] for c in range(4)]
        for s in range(VIEWS - 2, -1, -1):
            result = over([zrecv[s, c] for c in range(4)], result)
        for c in range(4):
            picture_ref[c, :half, :] = result[c][:, : cols // 2]
            picture_ref[c, half:, :] = pltpu.roll(result[c], cols // 2, 1)[:, : cols // 2]
        for v in range(VIEWS):
            pair_copies[v].wait_send()
            pl.when(myz != v)(group_copies[v].wait_send)

    leave(lat_copies)
    leave(edge_copies)
    leave(mid_copies)
    leave(corner_copies)
    for copy in outs:
        copy.wait()


def from_partner(shard, axis, apart):
    return lax.ppermute(shard, axis, [(i, i ^ 1 << apart) for i in range(lax.axis_size(axis))])


def over_blend(in_front, behind):
    return jnp.concatenate(
        [in_front[:3] + in_front[3:] * behind[:3], in_front[3:] * behind[3:]], axis=0
    )


def binary_swap(picture, depth_size):
    row_count, pixels = picture.shape[1:]
    bit_count = depth_size.bit_length() - 1
    block_width = pixels >> bit_count
    shaped = picture.reshape((4, row_count) + (2,) * bit_count + (block_width,))
    permuted = (0, 1) + tuple(range(bit_count + 1, 1, -1)) + (bit_count + 2,)
    picture = jnp.transpose(shaped, permuted).reshape(4, row_count, pixels)
    my_index = lax.axis_index("depth")
    for b in range(bit_count):
        half_width = picture.shape[2] // 2
        front_half = picture[:, :, :half_width]
        second = picture[:, :, half_width:]
        upper_bit = my_index >> b & 1 == 1
        kept_half = jnp.where(upper_bit, second, front_half)
        sent_half = jnp.where(upper_bit, front_half, second)
        partner = from_partner(sent_half, "depth", b)
        in_front = jnp.where(upper_bit, partner, kept_half)
        behind = jnp.where(upper_bit, kept_half, partner)
        picture = over_blend(in_front, behind)
    return picture


def per_device(phase, temper, iface_count):
    layers, rows, cols = phase.shape
    depth_size = lax.axis_size("depth")
    lat_size = lax.axis_size("lat")
    swap = depth_size == 2 * VIEWS
    width = cols // 2 if swap else VIEWS * cols
    grid = (2, layers + 2 * SWEEPS, rows + 2 * TILE, cols)
    tile = (VIEWS, 4, rows // 2, cols)
    dma = pltpu.SemaphoreType.DMA
    phase_next, heat_next, picture = pl.pallas_call(
        functools.partial(kernel, depth_size, lat_size, swap),
        out_shape=(
            jax.ShapeDtypeStruct(phase.shape, jnp.float32),
            jax.ShapeDtypeStruct(phase.shape, jnp.float32),
            jax.ShapeDtypeStruct((4, rows, width), jnp.float32),
        ),
        in_specs=[
            pl.BlockSpec(memory_space=pl.ANY),
            pl.BlockSpec(memory_space=pl.ANY),
            pl.BlockSpec(memory_space=pltpu.SMEM),
        ],
        out_specs=(
            pl.BlockSpec(memory_space=pl.ANY),
            pl.BlockSpec(memory_space=pl.ANY),
            pl.BlockSpec(memory_space=pltpu.VMEM),
        ),
        scratch_shapes=[pltpu.VMEM(grid, jnp.float32) for _ in range(5)]
        + [pltpu.VMEM(tile, jnp.float32) for _ in range(5)]
        + [
            dma((2,)),
            dma((2,)),
            dma((3, 2, 2)),
            dma((3, 2, 2)),
            dma((2, 2)),
            dma((2, 2)),
            dma((2, 2)),
            dma((2, 2)),
            dma((VIEWS,)),
            dma((VIEWS,)),
            dma((VIEWS,)),
            dma((VIEWS,)),
        ],
        compiler_params=pltpu.CompilerParams(
            collective_id=0, has_side_effects=True, vmem_limit_bytes=40 * 1024 * 1024
        ),
    )(phase, temper, iface_count)
    if not swap:
        picture = binary_swap(picture, depth_size)
    return phase_next, heat_next, picture


def solution(mesh):
    return jax.shard_map(
        per_device,
        mesh=mesh,
        in_specs=(P("depth", "lat", None), P("depth", "lat", None), P("depth", "lat")),
        out_specs=(P("depth", "lat", None), P("depth", "lat", None), P(None, "lat", "depth")),
        check_vma=False,
    )
```

```python
import functools
import math

import jax
import jax.numpy as jnp
import numpy as np
from jax import lax
from jax.experimental import pallas as pl
from jax.experimental.pallas import tpu as pltpu
from jax.sharding import PartitionSpec as P

SWEEPS = 3

DIFFUSION = (0.5, 2.0)
TIME_STEP = 0.4
COUPLE = 0.6
LATENT = 0.5
SHEAR_Y = (1.6, -1.6, 0.8, -1.2)
SHEAR_Z = (0.9, -0.6, -0.9, 0.3)
CENTERS = (-0.8, 0.0, 0.8)
VIEWS = len(SHEAR_Y)
MESH = pl.DeviceIdType.MESH
TILE = 8
REACH = 4


def thetas(sweep_total):
    chebyshev = []
    for f in range(2):
        highest = 1.0 + 12.0 * DIFFUSION[f]
        entries = [
            0.5 * (highest + 1.0)
            + 0.5 * (highest - 1.0) * math.cos((2 * j + 1) * math.pi / (2 * sweep_total))
            for j in range(sweep_total)
        ]
        chebyshev.append(entries)
    return np.array(chebyshev)


def over(front, behind):
    return [front[c] + front[3] * behind[c] for c in range(3)] + [front[3] * behind[3]]


def segments(x_lo, x_hi, shear, layers):
    runs = []
    for x in range(x_lo, x_hi):
        whole = int(math.floor(abs(shear) * x / layers))
        if runs and runs[-1][2] == whole:
            runs[-1][1] = x + 1
        else:
            runs.append([x, x + 1, whole])
    return runs


def blocked(lo, hi, step, body, carry):
    count = (hi - lo) // step

    def block(i, inner):
        return body([lo + i * step + j for j in range(step)], inner)

    if count:
        carry = lax.fori_loop(0, count, block, carry)
    rest = list(range(lo + count * step, hi))
    return body(rest, carry) if rest else carry


def kernel(
    depth_size,
    lat_size,
    swap,
    phase_ref,
    temper_ref,
    count_ref,
    phase_out,
    heat_out,
    picture_ref,
    u0,
    u1,
    u2,
    u3,
    src,
    keep,
    sent,
    xrecv,
    merged,
    zrecv,
    in_sem,
    out_sem,
    xs_sem,
    xr_sem,
    ys_sem,
    yr_sem,
    cs_sem,
    cr_sem,
    ps_sem,
    pr_sem,
    zs_sem,
    zr_sem,
):
    layers, rows, cols = phase_ref.shape
    halo = SWEEPS
    d = lax.axis_index("depth")
    l = lax.axis_index("lat")
    has_prev, has_next = d > 0, d < depth_size - 1
    has_low, has_high = l > 0, l < lat_size - 1
    up, down = lax.rem(d + 1, depth_size), lax.rem(d + depth_size - 1, depth_size)
    right, left = lax.rem(l + 1, lat_size), lax.rem(l + lat_size - 1, lat_size)
    xbit = lax.rem(d, 2)
    myz = d // 2
    partner = d + 1 - 2 * xbit
    fields = (phase_ref, temper_ref)

    local = [
        pltpu.make_async_copy(
            fields[f], u0.at[f, pl.ds(halo, layers), pl.ds(TILE, rows), :], in_sem.at[f]
        )
        for f in range(2)
    ]
    for copy in local:
        copy.start()

    barrier = pltpu.get_barrier_semaphore()
    greet = ((has_prev, (down, l)), (has_next, (up, l)), (has_low, (d, left)), (has_high, (d, right)))
    for there, device in greet:

        @pl.when(there)
        def _():
            pl.semaphore_signal(barrier, inc=1, device_id=device, device_id_type=MESH)

    if swap:
        for z in range(VIEWS):

            @pl.when(myz != z)
            def _():
                pl.semaphore_signal(
                    barrier, inc=1, device_id=(2 * z + xbit, l), device_id_type=MESH
                )

    @pl.when(d == 0)
    def _():
        u0[:, :halo] = jnp.zeros((2, halo, rows + 2 * TILE, cols), jnp.float32)

    @pl.when(d == depth_size - 1)
    def _():
        u0[:, halo + layers :] = jnp.zeros((2, halo, rows + 2 * TILE, cols), jnp.float32)

    for edge, first in ((l == 0, 0), (l == lat_size - 1, TILE + rows)):

        @pl.when(edge)
        def _():
            def clear(x, carry):
                for f in range(2):
                    u0[f, x, pl.ds(first, TILE), :] = jnp.zeros((TILE, cols), jnp.float32)
                return carry

            lax.fori_loop(0, layers + 2 * halo, clear, 0)

    peers = sum(
        jnp.minimum(n, 1) for n in (d, depth_size - 1 - d, l, lat_size - 1 - l)
    )
    pl.semaphore_wait(barrier, peers + (VIEWS - 1 if swap else 0))

    lat_copies, edge_copies, mid_copies, corner_copies = [], [], [], []
    for way in range(2):
        row_from, row_to = ((rows - TILE, 0), (0, TILE + rows))[way]
        for f in range(2):
            copy = pltpu.make_async_remote_copy(
                src_ref=fields[f].at[:, pl.ds(row_from, TILE), :],
                dst_ref=u0.at[f, pl.ds(halo, layers), pl.ds(row_to, TILE), :],
                send_sem=ys_sem.at[way, f],
                recv_sem=yr_sem.at[way, f],
                device_id=(d, (right, left)[way]),
                device_id_type=MESH,
            )
            lat_copies.append(((has_high, has_low)[way], (has_low, has_high)[way], copy))
    pieces = ((0, TILE), (rows - TILE, TILE), (TILE, rows - 2 * TILE))
    for piece, (row, size) in enumerate(pieces):
        for way in range(2):
            layer_from, layer_to = ((layers - halo, 0), (0, halo + layers))[way]
            for f in range(2):
                copy = pltpu.make_async_remote_copy(
                    src_ref=fields[f].at[pl.ds(layer_from, halo), pl.ds(row, size), :],
                    dst_ref=u0.at[f, pl.ds(layer_to, halo), pl.ds(TILE + row, size), :],
                    send_sem=xs_sem.at[piece, way, f],
                    recv_sem=xr_sem.at[piece, way, f],
                    device_id=((up, down)[way], l),
                    device_id_type=MESH,
                )
                entry = ((has_next, has_prev)[way], (has_prev, has_next)[way], copy)
                (mid_copies if piece == 2 else edge_copies).append(entry)
    for side in range(2):
        layer = (0, halo + layers)[side]
        filled = (has_prev, has_next)[side]
        for way in range(2):
            row_from, row_to = ((rows, 0), (TILE, TILE + rows))[way]
            copy = pltpu.make_async_remote_copy(
                src_ref=u0.at[:, pl.ds(layer, halo), pl.ds(row_from, TILE), :],
                dst_ref=u0.at[:, pl.ds(layer, halo), pl.ds(row_to, TILE), :],
                send_sem=cs_sem.at[side, way],
                recv_sem=cr_sem.at[side, way],
                device_id=(d, (right, left)[way]),
                device_id_type=MESH,
            )
            sends = jnp.logical_and(filled, (has_high, has_low)[way])
            receives = jnp.logical_and(filled, (has_low, has_high)[way])
            corner_copies.append((sends, receives, copy))

    def start(entries):
        for sends, _receives, copy in entries:
            pl.when(sends)(copy.start)

    def arrive(entries):
        for _sends, receives, copy in entries:
            pl.when(receives)(copy.wait_recv)

    def leave(entries):
        for sends, _receives, copy in entries:
            pl.when(sends)(copy.wait_send)

    start(edge_copies)
    start(lat_copies)
    start(mid_copies)
    for copy in local:
        copy.wait()
    arrive(lat_copies)

    chebyshev = thetas(SWEEPS)
    first_row = TILE - REACH
    span = rows + 2 * REACH
    chunk = next(n for n in (24, 16, 8) if span % n == 0)
    lane = lax.broadcasted_iota(jnp.int32, (chunk, cols), 1)
    row_id = lax.broadcasted_iota(jnp.int32, (chunk, cols), 0)
    low_mask = jnp.where(jnp.logical_or(row_id >= REACH, has_low), 1.0, 0.0)
    high_mask = jnp.where(jnp.logical_or(row_id < chunk - REACH, has_high), 1.0, 0.0)

    def sweep(k, before, after, x_lo, x_hi, edge):
        def body(xs, carry):
            results = []
            for x in xs:
                factor = None
                if edge:
                    inside = jnp.logical_and(
                        jnp.logical_or(x >= halo, has_prev),
                        jnp.logical_or(x < halo + layers, has_next),
                    )
                    factor = jnp.where(inside, 1.0, 0.0)
                for r0 in range(first_row, first_row + span, chunk):
                    here = pl.ds(r0, chunk)
                    values = [before[f, x, here, :] for f in range(2)]
                    if k == 0:
                        p, t = values
                        reaction = p * (1.0 - p) * (p - 0.5 + COUPLE * t)
                        sources = [p + TIME_STEP * reaction, t + LATENT * TIME_STEP * reaction]
                    else:
                        sources = [src[f, x, here, :] for f in range(2)]
                    for f in range(2):
                        u = values[f]
                        around = before[f, x - 1, here, :] + before[f, x + 1, here, :]
                        around = around + (
                            before[f, x, pl.ds(r0 - 1, chunk), :]
                            + before[f, x, pl.ds(r0 + 1, chunk), :]
                        )
                        around = around + (
                            jnp.where(lane == 0, 0.0, pltpu.roll(u, 1, 1))
                            + jnp.where(lane == cols - 1, 0.0, pltpu.roll(u, cols - 1, 1))
                        )
                        theta = chebyshev[f, k]
                        new = (
                            float(1.0 - (1.0 + 6.0 * DIFFUSION[f]) / theta) * u
                            + float(1.0 / theta) * sources[f]
                            + float(DIFFUSION[f] / theta) * around
                        )
                        if r0 == first_row:
                            new = new * low_mask
                        if r0 + chunk == first_row + span:
                            new = new * high_mask
                        if edge:
                            new = new * factor
                        results.append((after, f, x, here, new))
                        if k == 0:
                            results.append((src, f, x, here, sources[f]))
            for ref, f, x, here, value in results:
                ref[f, x, here, :] = value
            return carry

        blocked(x_lo, x_hi, 1 if k == 0 else 2, body, 0)

    stages = (u0, u1, u2, u3)
    total = layers + 2 * halo
    for k in range(SWEEPS):
        sweep(k, stages[k], stages[k + 1], halo + 1 + k, halo + layers - 1 - k, False)

    arrive(edge_copies)
    start(corner_copies)
    arrive(mid_copies)
    arrive(corner_copies)
    for k in range(SWEEPS):
        sweep(k, stages[k], stages[k + 1], 1 + k, halo + 1 + k, True)
        sweep(k, stages[k], stages[k + 1], halo + layers - 1 - k, total - 1 - k, True)

    outs = [
        pltpu.make_async_copy(
            u3.at[f, pl.ds(halo, layers), pl.ds(TILE, rows), :],
            (phase_out, heat_out)[f],
            out_sem.at[f],
        )
        for f in range(2)
    ]
    for copy in outs:
        copy.start()

    half = rows // 2
    count = count_ref[0, 0]
    lane1 = lax.broadcasted_iota(jnp.int32, (1, cols), 1)
    opacity = 4.0 / (layers * depth_size)

    def render(v, r0, x_lo, x_hi, carry):
        sy = 1 if SHEAR_Y[v] > 0 else -1
        sz = 1 if SHEAR_Z[v] > 0 else -1
        inside = jnp.where(lane1 == (cols - 1 if sz > 0 else 0), 0.0, 1.0)
        for lo, hi, whole in segments(x_lo, x_hi, SHEAR_Y[v], layers):

            def layer(x, carry, whole=whole):
                trans, red, green, blue = carry
                xf = lax.convert_element_type(x, jnp.float32)
                fy = xf * (abs(SHEAR_Y[v]) / layers) - whole
                fz = xf * (abs(SHEAR_Z[v]) / layers)
                far_z = inside * fz
                sampled = []
                for f in range(2):
                    near = u3[f, x + halo, pl.ds(TILE + r0 + sy * whole, half), :]
                    far = u3[f, x + halo, pl.ds(TILE + r0 + sy * (whole + 1), half), :]
                    b = near + fy * (far - near)
                    beside = pltpu.roll(b, cols - 1 if sz > 0 else 1, 1)
                    sampled.append((1.0 - fz) * b + far_z * beside)
                scale = jnp.where(x < count, -opacity, 0.0)
                after = trans * jnp.exp(scale * sampled[0] * sampled[0])
                weight = trans - after
                s = sampled[1]
                q = s * s
                d1 = q + 1.0
                a = q + (1.0 + CENTERS[2] * CENTERS[2])
                b = (2.0 * CENTERS[2]) * s
                d0, d2 = a + b, a - b
                sides = d0 * d2
                whole_product = sides * d1
                inverse = pl.reciprocal(whole_product, approx=True)
                inverse = inverse * (2.0 - whole_product * inverse)
                wr = weight * inverse
                wd = wr * d1
                return (after, red + wd * d2, green + wr * sides, blue + wd * d0)

            def body(xs, carry):
                for x in xs:
                    carry = layer(x, carry)
                return carry

            carry = blocked(lo, hi, 4, body, carry)
        return carry

    zero = jnp.zeros((half, cols), jnp.float32)
    one = jnp.ones((half, cols), jnp.float32)

    def picture_of(v):
        parts = []
        for r0 in (0, half):
            trans, red, green, blue = render(v, r0, 0, layers, (one, zero, zero, zero))
            parts.append([red, green, blue, trans])
        return parts

    if not swap:
        for v in range(VIEWS):
            for h, part in enumerate(picture_of(v)):
                for c in range(4):
                    picture_ref[c, h * half : (h + 1) * half, v * cols : (v + 1) * cols] = part[c]
    else:
        left_lanes = lax.broadcasted_iota(jnp.int32, (half, cols), 1) < cols // 2
        pair_copies = [
            pltpu.make_async_remote_copy(
                src_ref=sent.at[v],
                dst_ref=xrecv.at[v],
                send_sem=ps_sem.at[v],
                recv_sem=pr_sem.at[v],
                device_id=(partner, l),
                device_id_type=MESH,
            )
            for v in range(VIEWS)
        ]
        group_copies = [
            pltpu.make_async_remote_copy(
                src_ref=merged.at[v],
                dst_ref=zrecv.at[myz],
                send_sem=zs_sem.at[v],
                recv_sem=zr_sem.at[myz],
                device_id=(2 * v + xbit, l),
                device_id_type=MESH,
            )
            for v in range(VIEWS)
        ]

        def send_pair(v):
            lo, hi = picture_of(v)
            for c in range(4):
                lower = jnp.where(left_lanes, lo[c], pltpu.roll(hi[c], cols // 2, 1))
                upper = jnp.where(left_lanes, pltpu.roll(lo[c], cols // 2, 1), hi[c])
                keep[v, c] = jnp.where(xbit == 0, lower, upper)
                sent[v, c] = jnp.where(xbit == 0, upper, lower)
            pair_copies[v].start()

        def send_group(v):
            pair_copies[v].wait_recv()
            mine = [keep[v, c] for c in range(4)]
            other = [xrecv[v, c] for c in range(4)]
            front = [jnp.where(xbit == 0, m, o) for m, o in zip(mine, other)]
            behind = [jnp.where(xbit == 0, o, m) for m, o in zip(mine, other)]
            result = over(front, behind)

            @pl.when(myz == v)
            def _():
                for c in range(4):
                    zrecv[v, c] = result[c]

            @pl.when(myz != v)
            def _():
                for c in range(4):
                    merged[v, c] = result[c]
                group_copies[v].start()

        order = [0, VIEWS - 1] + list(range(1, VIEWS - 1))
        for place, v in enumerate(order):
            send_pair(v)
            if place:
                send_group(order[place - 1])
        send_group(order[-1])

        for s in range(VIEWS):

            @pl.when(myz != s)
            def _():
                pltpu.make_async_remote_copy(
                    src_ref=merged.at[s],
                    dst_ref=zrecv.at[s],
                    send_sem=zs_sem.at[s],
                    recv_sem=zr_sem.at[s],
                    device_id=(2 * s + xbit, l),
                    device_id_type=MESH,
                ).wait_recv()

        result = [zrecv[VIEWS - 1, c] for c in range(4)]
        for s in range(VIEWS - 2, -1, -1):
            result = over([zrecv[s, c] for c in range(4)], result)
        for c in range(4):
            picture_ref[c, :half, :] = result[c][:, : cols // 2]
            picture_ref[c, half:, :] = pltpu.roll(result[c], cols // 2, 1)[:, : cols // 2]
        for v in range(VIEWS):
            pair_copies[v].wait_send()
            pl.when(myz != v)(group_copies[v].wait_send)

    leave(lat_copies)
    leave(edge_copies)
    leave(mid_copies)
    leave(corner_copies)
    for copy in outs:
        copy.wait()


def from_partner(shard, axis, apart):
    return lax.ppermute(shard, axis, [(i, i ^ 1 << apart) for i in range(lax.axis_size(axis))])


def over_blend(in_front, behind):
    return jnp.concatenate(
        [in_front[:3] + in_front[3:] * behind[:3], in_front[3:] * behind[3:]], axis=0
    )


def binary_swap(picture, depth_size):
    row_count, pixels = picture.shape[1:]
    bit_count = depth_size.bit_length() - 1
    block_width = pixels >> bit_count
    shaped = picture.reshape((4, row_count) + (2,) * bit_count + (block_width,))
    permuted = (0, 1) + tuple(range(bit_count + 1, 1, -1)) + (bit_count + 2,)
    picture = jnp.transpose(shaped, permuted).reshape(4, row_count, pixels)
    my_index = lax.axis_index("depth")
    for b in range(bit_count):
        half_width = picture.shape[2] // 2
        front_half = picture[:, :, :half_width]
        second = picture[:, :, half_width:]
        upper_bit = my_index >> b & 1 == 1
        kept_half = jnp.where(upper_bit, second, front_half)
        sent_half = jnp.where(upper_bit, front_half, second)
        partner = from_partner(sent_half, "depth", b)
        in_front = jnp.where(upper_bit, partner, kept_half)
        behind = jnp.where(upper_bit, kept_half, partner)
        picture = over_blend(in_front, behind)
    return picture


def per_device(phase, temper, iface_count):
    layers, rows, cols = phase.shape
    depth_size = lax.axis_size("depth")
    lat_size = lax.axis_size("lat")
    swap = depth_size == 2 * VIEWS
    width = cols // 2 if swap else VIEWS * cols
    grid = (2, layers + 2 * SWEEPS, rows + 2 * TILE, cols)
    tile = (VIEWS, 4, rows // 2, cols)
    dma = pltpu.SemaphoreType.DMA
    phase_next, heat_next, picture = pl.pallas_call(
        functools.partial(kernel, depth_size, lat_size, swap),
        out_shape=(
            jax.ShapeDtypeStruct(phase.shape, jnp.float32),
            jax.ShapeDtypeStruct(phase.shape, jnp.float32),
            jax.ShapeDtypeStruct((4, rows, width), jnp.float32),
        ),
        in_specs=[
            pl.BlockSpec(memory_space=pl.ANY),
            pl.BlockSpec(memory_space=pl.ANY),
            pl.BlockSpec(memory_space=pltpu.SMEM),
        ],
        out_specs=(
            pl.BlockSpec(memory_space=pl.ANY),
            pl.BlockSpec(memory_space=pl.ANY),
            pl.BlockSpec(memory_space=pltpu.VMEM),
        ),
        scratch_shapes=[pltpu.VMEM(grid, jnp.float32) for _ in range(5)]
        + [pltpu.VMEM(tile, jnp.float32) for _ in range(5)]
        + [
            dma((2,)),
            dma((2,)),
            dma((3, 2, 2)),
            dma((3, 2, 2)),
            dma((2, 2)),
            dma((2, 2)),
            dma((2, 2)),
            dma((2, 2)),
            dma((VIEWS,)),
            dma((VIEWS,)),
            dma((VIEWS,)),
            dma((VIEWS,)),
        ],
        compiler_params=pltpu.CompilerParams(
            collective_id=0, has_side_effects=True, vmem_limit_bytes=60 * 1024 * 1024
        ),
    )(phase, temper, iface_count)
    if not swap:
        picture = binary_swap(picture, depth_size)
    return phase_next, heat_next, picture


def solution(mesh):
    return jax.shard_map(
        per_device,
        mesh=mesh,
        in_specs=(P("depth", "lat", None), P("depth", "lat", None), P("depth", "lat")),
        out_specs=(P("depth", "lat", None), P("depth", "lat", None), P(None, "lat", "depth")),
        check_vma=False,
    )
```

```python
import functools
import math

import jax
import jax.numpy as jnp
import numpy as np
from jax import lax
from jax.experimental import pallas as pl
from jax.experimental.pallas import tpu as pltpu
from jax.sharding import PartitionSpec as P

SWEEPS = 3

DIFFUSION = (0.5, 2.0)
TIME_STEP = 0.4
COUPLE = 0.6
LATENT = 0.5
SHEAR_Y = (1.6, -1.6, 0.8, -1.2)
SHEAR_Z = (0.9, -0.6, -0.9, 0.3)
CENTERS = (-0.8, 0.0, 0.8)
VIEWS = len(SHEAR_Y)
MESH = pl.DeviceIdType.MESH
TILE = 8
REACH = 4
GROUPS = 4
EARLY = 2


def thetas(sweep_total):
    chebyshev = []
    for f in range(2):
        highest = 1.0 + 12.0 * DIFFUSION[f]
        entries = [
            0.5 * (highest + 1.0)
            + 0.5 * (highest - 1.0) * math.cos((2 * j + 1) * math.pi / (2 * sweep_total))
            for j in range(sweep_total)
        ]
        chebyshev.append(entries)
    return np.array(chebyshev)


def over(front, behind):
    return [front[c] + front[3] * behind[c] for c in range(3)] + [front[3] * behind[3]]


def segments(x_lo, x_hi, shear, layers):
    runs = []
    for x in range(x_lo, x_hi):
        whole = int(math.floor(abs(shear) * x / layers))
        if runs and runs[-1][2] == whole:
            runs[-1][1] = x + 1
        else:
            runs.append([x, x + 1, whole])
    return runs


def blocked(lo, hi, step, body, carry):
    count = (hi - lo) // step

    def block(i, inner):
        return body([lo + i * step + j for j in range(step)], inner)

    if count:
        carry = lax.fori_loop(0, count, block, carry)
    rest = list(range(lo + count * step, hi))
    return body(rest, carry) if rest else carry


def kernel(
    depth_size,
    lat_size,
    swap,
    phase_ref,
    temper_ref,
    count_ref,
    phase_out,
    heat_out,
    picture_ref,
    u0,
    u1,
    u2,
    u3,
    src,
    stash,
    keep,
    sent,
    xrecv,
    merged,
    zrecv,
    in_sem,
    out_sem,
    xs_sem,
    xr_sem,
    ys_sem,
    yr_sem,
    cs_sem,
    cr_sem,
    ps_sem,
    pr_sem,
    zs_sem,
    zr_sem,
):
    layers, rows, cols = phase_ref.shape
    halo = SWEEPS
    d = lax.axis_index("depth")
    l = lax.axis_index("lat")
    has_prev, has_next = d > 0, d < depth_size - 1
    has_low, has_high = l > 0, l < lat_size - 1
    up, down = lax.rem(d + 1, depth_size), lax.rem(d + depth_size - 1, depth_size)
    right, left = lax.rem(l + 1, lat_size), lax.rem(l + lat_size - 1, lat_size)
    xbit = lax.rem(d, 2)
    myz = d // 2
    partner = d + 1 - 2 * xbit
    fields = (phase_ref, temper_ref)

    local = [
        pltpu.make_async_copy(
            fields[f], u0.at[f, pl.ds(halo, layers), pl.ds(TILE, rows), :], in_sem.at[f]
        )
        for f in range(2)
    ]
    for copy in local:
        copy.start()

    barrier = pltpu.get_barrier_semaphore()
    greet = ((has_prev, (down, l)), (has_next, (up, l)), (has_low, (d, left)), (has_high, (d, right)))
    for there, device in greet:

        @pl.when(there)
        def _():
            pl.semaphore_signal(barrier, inc=1, device_id=device, device_id_type=MESH)

    if swap:
        for z in range(VIEWS):

            @pl.when(myz != z)
            def _():
                pl.semaphore_signal(
                    barrier, inc=1, device_id=(2 * z + xbit, l), device_id_type=MESH
                )

    @pl.when(d == 0)
    def _():
        u0[:, :halo] = jnp.zeros((2, halo, rows + 2 * TILE, cols), jnp.float32)

    @pl.when(d == depth_size - 1)
    def _():
        u0[:, halo + layers :] = jnp.zeros((2, halo, rows + 2 * TILE, cols), jnp.float32)

    for edge, first in ((l == 0, 0), (l == lat_size - 1, TILE + rows)):

        @pl.when(edge)
        def _():
            def clear(x, carry):
                for f in range(2):
                    u0[f, x, pl.ds(first, TILE), :] = jnp.zeros((TILE, cols), jnp.float32)
                return carry

            lax.fori_loop(0, layers + 2 * halo, clear, 0)

    peers = sum(
        jnp.minimum(n, 1) for n in (d, depth_size - 1 - d, l, lat_size - 1 - l)
    )
    pl.semaphore_wait(barrier, peers + (VIEWS - 1 if swap else 0))

    lat_copies, edge_copies, mid_copies, corner_copies = [], [], [], []
    groups = GROUPS if layers % GROUPS == 0 else 1
    depth = layers // groups
    for g in range(groups):
        lat_copies.append([])
        for way in range(2):
            row_from, row_to = ((rows - TILE, 0), (0, TILE + rows))[way]
            for f in range(2):
                copy = pltpu.make_async_remote_copy(
                    src_ref=fields[f].at[pl.ds(g * depth, depth), pl.ds(row_from, TILE), :],
                    dst_ref=u0.at[f, pl.ds(halo + g * depth, depth), pl.ds(row_to, TILE), :],
                    send_sem=ys_sem.at[g, way, f],
                    recv_sem=yr_sem.at[g, way, f],
                    device_id=(d, (right, left)[way]),
                    device_id_type=MESH,
                )
                entry = ((has_high, has_low)[way], (has_low, has_high)[way], copy)
                lat_copies[g].append(entry)
    pieces = ((0, TILE), (rows - TILE, TILE), (TILE, rows - 2 * TILE))
    for piece, (row, size) in enumerate(pieces):
        for way in range(2):
            layer_from, layer_to = ((layers - halo, 0), (0, halo + layers))[way]
            for f in range(2):
                copy = pltpu.make_async_remote_copy(
                    src_ref=fields[f].at[pl.ds(layer_from, halo), pl.ds(row, size), :],
                    dst_ref=u0.at[f, pl.ds(layer_to, halo), pl.ds(TILE + row, size), :],
                    send_sem=xs_sem.at[piece, way, f],
                    recv_sem=xr_sem.at[piece, way, f],
                    device_id=((up, down)[way], l),
                    device_id_type=MESH,
                )
                entry = ((has_next, has_prev)[way], (has_prev, has_next)[way], copy)
                (mid_copies if piece == 2 else edge_copies).append(entry)
    for side in range(2):
        layer = (0, halo + layers)[side]
        filled = (has_prev, has_next)[side]
        for way in range(2):
            row_from, row_to = ((rows, 0), (TILE, TILE + rows))[way]
            copy = pltpu.make_async_remote_copy(
                src_ref=u0.at[:, pl.ds(layer, halo), pl.ds(row_from, TILE), :],
                dst_ref=u0.at[:, pl.ds(layer, halo), pl.ds(row_to, TILE), :],
                send_sem=cs_sem.at[side, way],
                recv_sem=cr_sem.at[side, way],
                device_id=(d, (right, left)[way]),
                device_id_type=MESH,
            )
            sends = jnp.logical_and(filled, (has_high, has_low)[way])
            receives = jnp.logical_and(filled, (has_low, has_high)[way])
            corner_copies.append((sends, receives, copy))

    def start(entries):
        for sends, _receives, copy in entries:
            pl.when(sends)(copy.start)

    def arrive(entries):
        for _sends, receives, copy in entries:
            pl.when(receives)(copy.wait_recv)

    def leave(entries):
        for sends, _receives, copy in entries:
            pl.when(sends)(copy.wait_send)

    start(edge_copies)
    start(lat_copies[0])
    start(mid_copies)
    for g in range(1, groups):
        start(lat_copies[g])
    for copy in local:
        copy.wait()

    chebyshev = thetas(SWEEPS)
    first_row = TILE - REACH
    span = rows + 2 * REACH
    chunk = next(n for n in (24, 16, 8) if span % n == 0)
    lane = lax.broadcasted_iota(jnp.int32, (chunk, cols), 1)
    row_id = lax.broadcasted_iota(jnp.int32, (chunk, cols), 0)
    low_mask = jnp.where(jnp.logical_or(row_id >= REACH, has_low), 1.0, 0.0)
    high_mask = jnp.where(jnp.logical_or(row_id < chunk - REACH, has_high), 1.0, 0.0)

    def sweep(k, before, after, x_lo, x_hi, edge):
        def body(xs, carry):
            results = []
            for x in xs:
                factor = None
                if edge:
                    inside = jnp.logical_and(
                        jnp.logical_or(x >= halo, has_prev),
                        jnp.logical_or(x < halo + layers, has_next),
                    )
                    factor = jnp.where(inside, 1.0, 0.0)
                for r0 in range(first_row, first_row + span, chunk):
                    here = pl.ds(r0, chunk)
                    values = [before[f, x, here, :] for f in range(2)]
                    if k == 0:
                        p, t = values
                        reaction = p * (1.0 - p) * (p - 0.5 + COUPLE * t)
                        sources = [p + TIME_STEP * reaction, t + LATENT * TIME_STEP * reaction]
                    else:
                        sources = [src[f, x, here, :] for f in range(2)]
                    for f in range(2):
                        u = values[f]
                        around = before[f, x - 1, here, :] + before[f, x + 1, here, :]
                        around = around + (
                            before[f, x, pl.ds(r0 - 1, chunk), :]
                            + before[f, x, pl.ds(r0 + 1, chunk), :]
                        )
                        around = around + (
                            jnp.where(lane == 0, 0.0, pltpu.roll(u, 1, 1))
                            + jnp.where(lane == cols - 1, 0.0, pltpu.roll(u, cols - 1, 1))
                        )
                        theta = chebyshev[f, k]
                        new = (
                            float(1.0 - (1.0 + 6.0 * DIFFUSION[f]) / theta) * u
                            + float(1.0 / theta) * sources[f]
                            + float(DIFFUSION[f] / theta) * around
                        )
                        if r0 == first_row:
                            new = new * low_mask
                        if r0 + chunk == first_row + span:
                            new = new * high_mask
                        if edge:
                            new = new * factor
                        results.append((after, f, x, here, new))
                        if k == 0:
                            results.append((src, f, x, here, sources[f]))
            for ref, f, x, here, value in results:
                ref[f, x, here, :] = value
            return carry

        blocked(x_lo, x_hi, 1 if k == 0 else 2, body, 0)

    stages = (u0, u1, u2, u3)
    total = layers + 2 * halo
    ready = halo + 1
    for g in range(groups):
        arrive(lat_copies[g])
        until = halo + (g + 1) * depth - 1
        sweep(0, u0, u1, ready, until, False)
        ready = until
    for k in range(1, SWEEPS):
        sweep(k, stages[k], stages[k + 1], halo + 1 + k, halo + layers - 1 - k, False)

    half = rows // 2
    count = count_ref[0, 0]
    lane1 = lax.broadcasted_iota(jnp.int32, (1, cols), 1)
    opacity = 4.0 / (layers * depth_size)

    def render(v, r0, x_lo, x_hi, carry):
        sy = 1 if SHEAR_Y[v] > 0 else -1
        sz = 1 if SHEAR_Z[v] > 0 else -1
        inside = jnp.where(lane1 == (cols - 1 if sz > 0 else 0), 0.0, 1.0)
        for lo, hi, whole in segments(x_lo, x_hi, SHEAR_Y[v], layers):

            def layer(x, carry, whole=whole):
                trans, red, green, blue = carry
                xf = lax.convert_element_type(x, jnp.float32)
                fy = xf * (abs(SHEAR_Y[v]) / layers) - whole
                fz = xf * (abs(SHEAR_Z[v]) / layers)
                far_z = inside * fz
                sampled = []
                for f in range(2):
                    near = u3[f, x + halo, pl.ds(TILE + r0 + sy * whole, half), :]
                    far = u3[f, x + halo, pl.ds(TILE + r0 + sy * (whole + 1), half), :]
                    b = near + fy * (far - near)
                    beside = pltpu.roll(b, cols - 1 if sz > 0 else 1, 1)
                    sampled.append((1.0 - fz) * b + far_z * beside)
                scale = jnp.where(x < count, -opacity, 0.0)
                after = trans * jnp.exp(scale * sampled[0] * sampled[0])
                weight = trans - after
                s = sampled[1]
                q = s * s
                d1 = q + 1.0
                a = q + (1.0 + CENTERS[2] * CENTERS[2])
                b = (2.0 * CENTERS[2]) * s
                d0, d2 = a + b, a - b
                sides = d0 * d2
                whole_product = sides * d1
                inverse = pl.reciprocal(whole_product, approx=True)
                wr = weight * inverse
                wd = wr * d1
                return (after, red + wd * d2, green + wr * sides, blue + wd * d0)

            def body(xs, carry):
                for x in xs:
                    carry = layer(x, carry)
                return carry

            carry = blocked(lo, hi, 4, body, carry)
        return carry

    zero = jnp.zeros((half, cols), jnp.float32)
    one = jnp.ones((half, cols), jnp.float32)

    start_carry = (one, zero, zero, zero)
    order = [0, VIEWS - 1] + list(range(1, VIEWS - 1))
    units = [(v, h) for v in order for h in range(2)]
    for place in range(EARLY):
        v, h = units[place]
        inner = render(v, h * half, halo, layers - halo, start_carry)
        for c in range(4):
            stash[place, c] = inner[c]

    arrive(edge_copies)
    start(corner_copies)
    arrive(mid_copies)
    arrive(corner_copies)
    for k in range(SWEEPS):
        sweep(k, stages[k], stages[k + 1], 1 + k, halo + 1 + k, True)
        sweep(k, stages[k], stages[k + 1], halo + layers - 1 - k, total - 1 - k, True)

    outs = [
        pltpu.make_async_copy(
            u3.at[f, pl.ds(halo, layers), pl.ds(TILE, rows), :],
            (phase_out, heat_out)[f],
            out_sem.at[f],
        )
        for f in range(2)
    ]
    for copy in outs:
        copy.start()

    def piece_of(place):
        v, h = units[place]
        if place < EARLY:
            trans, *colours = render(v, h * half, 0, halo, start_carry)
            inner = [stash[place, c] for c in range(4)]
            carry = (trans * inner[0],) + tuple(
                colours[c] + trans * inner[1 + c] for c in range(3)
            )
            carry = render(v, h * half, layers - halo, layers, carry)
        else:
            carry = render(v, h * half, 0, layers, start_carry)
        trans, red, green, blue = carry
        return [red, green, blue, trans]

    if not swap:
        for place, (v, h) in enumerate(units):
            part = piece_of(place)
            for c in range(4):
                picture_ref[c, h * half : (h + 1) * half, v * cols : (v + 1) * cols] = part[c]
    else:
        quarter = half // 2
        left_lanes = lax.broadcasted_iota(jnp.int32, (quarter, cols), 1) < cols // 2

        def pair_copy(v, h):
            return pltpu.make_async_remote_copy(
                src_ref=sent.at[v, h],
                dst_ref=xrecv.at[v, h],
                send_sem=ps_sem.at[v, h],
                recv_sem=pr_sem.at[v, h],
                device_id=(partner, l),
                device_id_type=MESH,
            )

        def group_copy(v, h, slot):
            return pltpu.make_async_remote_copy(
                src_ref=merged.at[v, h],
                dst_ref=zrecv.at[slot, h],
                send_sem=zs_sem.at[v, h],
                recv_sem=zr_sem.at[slot, h],
                device_id=(2 * v + xbit, l),
                device_id_type=MESH,
            )

        def send_pair(place):
            v, h = units[place]
            part = piece_of(place)
            for c in range(4):
                lo, hi = part[c][:quarter], part[c][quarter:]
                lower = jnp.where(left_lanes, lo, pltpu.roll(hi, cols // 2, 1))
                upper = jnp.where(left_lanes, pltpu.roll(lo, cols // 2, 1), hi)
                keep[v, h, c] = jnp.where(xbit == 0, lower, upper)
                sent[v, h, c] = jnp.where(xbit == 0, upper, lower)
            pair_copy(v, h).start()

        def send_group(place):
            v, h = units[place]
            pair_copy(v, h).wait_recv()
            mine = [keep[v, h, c] for c in range(4)]
            other = [xrecv[v, h, c] for c in range(4)]
            front = [jnp.where(xbit == 0, m, o) for m, o in zip(mine, other)]
            behind = [jnp.where(xbit == 0, o, m) for m, o in zip(mine, other)]
            result = over(front, behind)

            @pl.when(myz == v)
            def _():
                for c in range(4):
                    zrecv[v, h, c] = result[c]

            @pl.when(myz != v)
            def _():
                for c in range(4):
                    merged[v, h, c] = result[c]
                group_copy(v, h, myz).start()

        for place in range(len(units)):
            send_pair(place)
            if place:
                send_group(place - 1)
        send_group(len(units) - 1)

        for h in range(2):
            for s in range(VIEWS):
                pl.when(myz != s)(group_copy(s, h, s).wait_recv)
            result = [zrecv[VIEWS - 1, h, c] for c in range(4)]
            for s in range(VIEWS - 2, -1, -1):
                result = over([zrecv[s, h, c] for c in range(4)], result)
            for c in range(4):
                picture_ref[h, c] = result[c]
        for v, h in units:
            pair_copy(v, h).wait_send()
            pl.when(myz != v)(group_copy(v, h, myz).wait_send)

    for entries in lat_copies:
        leave(entries)
    leave(edge_copies)
    leave(mid_copies)
    leave(corner_copies)
    for copy in outs:
        copy.wait()


def deliver(phase_ref, heat_ref, packed_ref, phase_out, heat_out, picture_ref, sem):
    copies = [
        pltpu.make_async_copy(phase_ref, phase_out, sem.at[0]),
        pltpu.make_async_copy(heat_ref, heat_out, sem.at[1]),
    ]
    for copy in copies:
        copy.start()
    halves, channels, quarter, cols = packed_ref.shape
    for h in range(halves):
        for c in range(channels):
            part = packed_ref[h, c]
            first = 2 * h * quarter
            picture_ref[c, first : first + quarter, :] = part[:, : cols // 2]
            picture_ref[c, first + quarter : first + 2 * quarter, :] = pltpu.roll(
                part, cols // 2, 1
            )[:, : cols // 2]
    for copy in copies:
        copy.wait()


def from_partner(shard, axis, apart):
    return lax.ppermute(shard, axis, [(i, i ^ 1 << apart) for i in range(lax.axis_size(axis))])


def over_blend(in_front, behind):
    return jnp.concatenate(
        [in_front[:3] + in_front[3:] * behind[:3], in_front[3:] * behind[3:]], axis=0
    )


def binary_swap(picture, depth_size):
    row_count, pixels = picture.shape[1:]
    bit_count = depth_size.bit_length() - 1
    block_width = pixels >> bit_count
    shaped = picture.reshape((4, row_count) + (2,) * bit_count + (block_width,))
    permuted = (0, 1) + tuple(range(bit_count + 1, 1, -1)) + (bit_count + 2,)
    picture = jnp.transpose(shaped, permuted).reshape(4, row_count, pixels)
    my_index = lax.axis_index("depth")
    for b in range(bit_count):
        half_width = picture.shape[2] // 2
        front_half = picture[:, :, :half_width]
        second = picture[:, :, half_width:]
        upper_bit = my_index >> b & 1 == 1
        kept_half = jnp.where(upper_bit, second, front_half)
        sent_half = jnp.where(upper_bit, front_half, second)
        partner = from_partner(sent_half, "depth", b)
        in_front = jnp.where(upper_bit, partner, kept_half)
        behind = jnp.where(upper_bit, kept_half, partner)
        picture = over_blend(in_front, behind)
    return picture


def per_device(phase, temper, iface_count):
    layers, rows, cols = phase.shape
    depth_size = lax.axis_size("depth")
    lat_size = lax.axis_size("lat")
    swap = depth_size == 2 * VIEWS
    packed = (2, 4, rows // 4, cols)
    piece = packed if swap else (4, rows, VIEWS * cols)
    grid = (2, layers + 2 * SWEEPS, rows + 2 * TILE, cols)
    tile = (VIEWS,) + packed
    dma = pltpu.SemaphoreType.DMA
    phase_next, heat_next, picture = pl.pallas_call(
        functools.partial(kernel, depth_size, lat_size, swap),
        out_shape=(
            jax.ShapeDtypeStruct(phase.shape, jnp.float32),
            jax.ShapeDtypeStruct(phase.shape, jnp.float32),
            jax.ShapeDtypeStruct(piece, jnp.float32),
        ),
        in_specs=[
            pl.BlockSpec(memory_space=pl.ANY),
            pl.BlockSpec(memory_space=pl.ANY),
            pl.BlockSpec(memory_space=pltpu.SMEM),
        ],
        out_specs=(
            pl.BlockSpec(memory_space=pl.ANY),
            pl.BlockSpec(memory_space=pl.ANY),
            pl.BlockSpec(memory_space=pltpu.VMEM),
        ),
        scratch_shapes=[pltpu.VMEM(grid, jnp.float32) for _ in range(5)]
        + [pltpu.VMEM((EARLY, 4, rows // 2, cols), jnp.float32)]
        + [pltpu.VMEM(tile, jnp.float32) for _ in range(5)]
        + [
            dma((2,)),
            dma((2,)),
            dma((3, 2, 2)),
            dma((3, 2, 2)),
            dma((GROUPS, 2, 2)),
            dma((GROUPS, 2, 2)),
            dma((2, 2)),
            dma((2, 2)),
            dma((VIEWS, 2)),
            dma((VIEWS, 2)),
            dma((VIEWS, 2)),
            dma((VIEWS, 2)),
        ],
        compiler_params=pltpu.CompilerParams(
            collective_id=0, has_side_effects=True, vmem_limit_bytes=60 * 1024 * 1024
        ),
    )(phase, temper, iface_count)
    if not swap:
        return phase_next, heat_next, binary_swap(picture, depth_size)
    return pl.pallas_call(
        deliver,
        out_shape=(
            jax.ShapeDtypeStruct(phase.shape, jnp.float32),
            jax.ShapeDtypeStruct(phase.shape, jnp.float32),
            jax.ShapeDtypeStruct((4, rows, cols // 2), jnp.float32),
        ),
        in_specs=[
            pl.BlockSpec(memory_space=pl.ANY),
            pl.BlockSpec(memory_space=pl.ANY),
            pl.BlockSpec(memory_space=pltpu.VMEM),
        ],
        out_specs=(
            pl.BlockSpec(memory_space=pl.ANY),
            pl.BlockSpec(memory_space=pl.ANY),
            pl.BlockSpec(memory_space=pltpu.VMEM),
        ),
        scratch_shapes=[dma((2,))],
    )(phase_next, heat_next, picture)


def solution(mesh):
    return jax.shard_map(
        per_device,
        mesh=mesh,
        in_specs=(P("depth", "lat", None), P("depth", "lat", None), P("depth", "lat")),
        out_specs=(P("depth", "lat", None), P("depth", "lat", None), P(None, "lat", "depth")),
        check_vma=False,
    )
```

```python
import functools
import math

import jax
import jax.numpy as jnp
import numpy as np
from jax import lax
from jax.experimental import pallas as pl
from jax.experimental.pallas import tpu as pltpu
from jax.sharding import PartitionSpec as P

SWEEPS = 3

DIFFUSION = (0.5, 2.0)
TIME_STEP = 0.4
COUPLE = 0.6
LATENT = 0.5
SHEAR_Y = (1.6, -1.6, 0.8, -1.2)
SHEAR_Z = (0.9, -0.6, -0.9, 0.3)
CENTERS = (-0.8, 0.0, 0.8)
VIEWS = len(SHEAR_Y)
MESH = pl.DeviceIdType.MESH
TILE = 8
REACH = 4
GROUPS = 4
CHUNKS = 8
STEP = 8
EARLY = 1


def thetas(sweep_total):
    chebyshev = []
    for f in range(2):
        highest = 1.0 + 12.0 * DIFFUSION[f]
        entries = [
            0.5 * (highest + 1.0)
            + 0.5 * (highest - 1.0) * math.cos((2 * j + 1) * math.pi / (2 * sweep_total))
            for j in range(sweep_total)
        ]
        chebyshev.append(entries)
    return np.array(chebyshev)


def over(front, behind):
    return [front[c] + front[3] * behind[c] for c in range(3)] + [front[3] * behind[3]]


def segments(x_lo, x_hi, shear, layers):
    runs = []
    for x in range(x_lo, x_hi):
        whole = int(math.floor(abs(shear) * x / layers))
        if runs and runs[-1][2] == whole:
            runs[-1][1] = x + 1
        else:
            runs.append([x, x + 1, whole])
    return runs


def blocked(lo, hi, step, body, carry):
    count = (hi - lo) // step

    def block(i, inner):
        return body([lo + i * step + j for j in range(step)], inner)

    if count:
        carry = lax.fori_loop(0, count, block, carry)
    rest = list(range(lo + count * step, hi))
    return body(rest, carry) if rest else carry


def kernel(
    depth_size,
    lat_size,
    swap,
    phase_ref,
    temper_ref,
    count_ref,
    phase_out,
    heat_out,
    picture_ref,
    u0,
    u1,
    u2,
    u3,
    src,
    stash,
    keep,
    sent,
    xrecv,
    merged,
    zrecv,
    in_sem,
    out_sem,
    xs_sem,
    xr_sem,
    ys_sem,
    yr_sem,
    cs_sem,
    cr_sem,
    ps_sem,
    pr_sem,
    zs_sem,
    zr_sem,
):
    layers, rows, cols = phase_ref.shape
    halo = SWEEPS
    d = lax.axis_index("depth")
    l = lax.axis_index("lat")
    has_prev, has_next = d > 0, d < depth_size - 1
    has_low, has_high = l > 0, l < lat_size - 1
    up, down = lax.rem(d + 1, depth_size), lax.rem(d + depth_size - 1, depth_size)
    right, left = lax.rem(l + 1, lat_size), lax.rem(l + lat_size - 1, lat_size)
    xbit = lax.rem(d, 2)
    myz = d // 2
    partner = d + 1 - 2 * xbit
    fields = (phase_ref, temper_ref)

    local = [
        pltpu.make_async_copy(
            fields[f], u0.at[f, pl.ds(halo, layers), pl.ds(TILE, rows), :], in_sem.at[f]
        )
        for f in range(2)
    ]
    for copy in local:
        copy.start()

    barrier = pltpu.get_barrier_semaphore()
    greet = ((has_prev, (down, l)), (has_next, (up, l)), (has_low, (d, left)), (has_high, (d, right)))
    for there, device in greet:

        @pl.when(there)
        def _():
            pl.semaphore_signal(barrier, inc=1, device_id=device, device_id_type=MESH)

    if swap:
        for z in range(VIEWS):

            @pl.when(myz != z)
            def _():
                pl.semaphore_signal(
                    barrier, inc=1, device_id=(2 * z + xbit, l), device_id_type=MESH
                )

    @pl.when(d == 0)
    def _():
        u0[:, :halo] = jnp.zeros((2, halo, rows + 2 * TILE, cols), jnp.float32)

    @pl.when(d == depth_size - 1)
    def _():
        u0[:, halo + layers :] = jnp.zeros((2, halo, rows + 2 * TILE, cols), jnp.float32)

    for edge, first in ((l == 0, 0), (l == lat_size - 1, TILE + rows)):

        @pl.when(edge)
        def _():
            def clear(x, carry):
                for f in range(2):
                    u0[f, x, pl.ds(first, TILE), :] = jnp.zeros((TILE, cols), jnp.float32)
                return carry

            lax.fori_loop(0, layers + 2 * halo, clear, 0)

    peers = sum(
        jnp.minimum(n, 1) for n in (d, depth_size - 1 - d, l, lat_size - 1 - l)
    )
    pl.semaphore_wait(barrier, peers + (VIEWS - 1 if swap else 0))

    lat_copies, edge_copies, mid_copies, corner_copies = [], [], [], []
    groups = GROUPS if layers % GROUPS == 0 else 1
    depth = layers // groups
    for g in range(groups):
        lat_copies.append([])
        for way in range(2):
            row_from, row_to = ((rows - TILE, 0), (0, TILE + rows))[way]
            for f in range(2):
                copy = pltpu.make_async_remote_copy(
                    src_ref=fields[f].at[pl.ds(g * depth, depth), pl.ds(row_from, TILE), :],
                    dst_ref=u0.at[f, pl.ds(halo + g * depth, depth), pl.ds(row_to, TILE), :],
                    send_sem=ys_sem.at[g, way, f],
                    recv_sem=yr_sem.at[g, way, f],
                    device_id=(d, (right, left)[way]),
                    device_id_type=MESH,
                )
                entry = ((has_high, has_low)[way], (has_low, has_high)[way], copy)
                lat_copies[g].append(entry)
    pieces = ((0, TILE), (rows - TILE, TILE), (TILE, rows - 2 * TILE))
    for piece, (row, size) in enumerate(pieces):
        for way in range(2):
            layer_from, layer_to = ((layers - halo, 0), (0, halo + layers))[way]
            for f in range(2):
                copy = pltpu.make_async_remote_copy(
                    src_ref=fields[f].at[pl.ds(layer_from, halo), pl.ds(row, size), :],
                    dst_ref=u0.at[f, pl.ds(layer_to, halo), pl.ds(TILE + row, size), :],
                    send_sem=xs_sem.at[piece, way, f],
                    recv_sem=xr_sem.at[piece, way, f],
                    device_id=((up, down)[way], l),
                    device_id_type=MESH,
                )
                entry = ((has_next, has_prev)[way], (has_prev, has_next)[way], copy)
                (mid_copies if piece == 2 else edge_copies).append(entry)
    for side in range(2):
        layer = (0, halo + layers)[side]
        filled = (has_prev, has_next)[side]
        for way in range(2):
            row_from, row_to = ((rows, 0), (TILE, TILE + rows))[way]
            copy = pltpu.make_async_remote_copy(
                src_ref=u0.at[:, pl.ds(layer, halo), pl.ds(row_from, TILE), :],
                dst_ref=u0.at[:, pl.ds(layer, halo), pl.ds(row_to, TILE), :],
                send_sem=cs_sem.at[side, way],
                recv_sem=cr_sem.at[side, way],
                device_id=(d, (right, left)[way]),
                device_id_type=MESH,
            )
            sends = jnp.logical_and(filled, (has_high, has_low)[way])
            receives = jnp.logical_and(filled, (has_low, has_high)[way])
            corner_copies.append((sends, receives, copy))

    def start(entries):
        for sends, _receives, copy in entries:
            pl.when(sends)(copy.start)

    def arrive(entries):
        for _sends, receives, copy in entries:
            pl.when(receives)(copy.wait_recv)

    def leave(entries):
        for sends, _receives, copy in entries:
            pl.when(sends)(copy.wait_send)

    start(edge_copies)
    start(lat_copies[0])
    start(mid_copies)
    for g in range(1, groups):
        start(lat_copies[g])
    for copy in local:
        copy.wait()

    chebyshev = thetas(SWEEPS)
    first_row = TILE - REACH
    span = rows + 2 * REACH
    chunk = next(n for n in (24, 16, 8) if span % n == 0)
    lane = lax.broadcasted_iota(jnp.int32, (chunk, cols), 1)
    row_id = lax.broadcasted_iota(jnp.int32, (chunk, cols), 0)
    low_mask = jnp.where(jnp.logical_or(row_id >= REACH, has_low), 1.0, 0.0)
    high_mask = jnp.where(jnp.logical_or(row_id < chunk - REACH, has_high), 1.0, 0.0)

    def sweep(k, before, after, x_lo, x_hi, edge):
        def body(xs, carry):
            results = []
            for x in xs:
                factor = None
                if edge:
                    inside = jnp.logical_and(
                        jnp.logical_or(x >= halo, has_prev),
                        jnp.logical_or(x < halo + layers, has_next),
                    )
                    factor = jnp.where(inside, 1.0, 0.0)
                for r0 in range(first_row, first_row + span, chunk):
                    here = pl.ds(r0, chunk)
                    values = [before[f, x, here, :] for f in range(2)]
                    if k == 0:
                        p, t = values
                        reaction = p * (1.0 - p) * (p - 0.5 + COUPLE * t)
                        sources = [p + TIME_STEP * reaction, t + LATENT * TIME_STEP * reaction]
                    else:
                        sources = [src[f, x, here, :] for f in range(2)]
                    for f in range(2):
                        u = values[f]
                        around = before[f, x - 1, here, :] + before[f, x + 1, here, :]
                        around = around + (
                            before[f, x, pl.ds(r0 - 1, chunk), :]
                            + before[f, x, pl.ds(r0 + 1, chunk), :]
                        )
                        around = around + (
                            jnp.where(lane == 0, 0.0, pltpu.roll(u, 1, 1))
                            + jnp.where(lane == cols - 1, 0.0, pltpu.roll(u, cols - 1, 1))
                        )
                        theta = chebyshev[f, k]
                        new = (
                            float(1.0 - (1.0 + 6.0 * DIFFUSION[f]) / theta) * u
                            + float(1.0 / theta) * sources[f]
                            + float(DIFFUSION[f] / theta) * around
                        )
                        if r0 == first_row:
                            new = new * low_mask
                        if r0 + chunk == first_row + span:
                            new = new * high_mask
                        if edge:
                            new = new * factor
                        results.append((after, f, x, here, new))
                        if k == 0:
                            results.append((src, f, x, here, sources[f]))
            for ref, f, x, here, value in results:
                ref[f, x, here, :] = value
            return carry

        blocked(x_lo, x_hi, 1 if k == 0 else 2, body, 0)

    stages = (u0, u1, u2, u3)
    total = layers + 2 * halo
    ready = halo + 1
    for g in range(groups):
        arrive(lat_copies[g])
        until = halo + (g + 1) * depth - 1
        sweep(0, u0, u1, ready, until, False)
        ready = until
    for k in range(1, SWEEPS):
        sweep(k, stages[k], stages[k + 1], halo + 1 + k, halo + layers - 1 - k, False)

    half = rows // 2
    count = count_ref[0, 0]
    lane1 = lax.broadcasted_iota(jnp.int32, (TILE, cols), 1)
    first_lane, last_lane = lane1 == 0, lane1 == cols - 1
    opacity = 4.0 / (layers * depth_size)
    starts = range(0, half, TILE)

    def render(v, r0, x_lo, x_hi, carry):
        sy = 1 if SHEAR_Y[v] > 0 else -1
        sz = 1 if SHEAR_Z[v] > 0 else -1
        edge_lane = last_lane if sz > 0 else first_lane

        def layer(x, whole, groups):
            xf = lax.convert_element_type(x, jnp.float32)
            fy = xf * (abs(SHEAR_Y[v]) / layers) - whole
            fz = xf * (abs(SHEAR_Z[v]) / layers)
            far_z = jnp.where(edge_lane, 0.0, fz)
            near_z = 1.0 - fz
            scale = jnp.where(x < count, -opacity, 0.0)
            result = []
            for row, (trans, red, green, blue) in zip(starts, groups):
                sampled = []
                for f in range(2):
                    first = TILE + r0 + row
                    near = u3[f, x + halo, pl.ds(first + sy * whole, TILE), :]
                    far = u3[f, x + halo, pl.ds(first + sy * (whole + 1), TILE), :]
                    b = near + fy * (far - near)
                    beside = pltpu.roll(b, cols - 1 if sz > 0 else 1, 1)
                    sampled.append(near_z * b + far_z * beside)
                after = trans * jnp.exp(scale * (sampled[0] * sampled[0]))
                weight = trans - after
                s = sampled[1]
                q = s * s
                d1 = q + 1.0
                a = q + (1.0 + CENTERS[2] * CENTERS[2])
                b = (2.0 * CENTERS[2]) * s
                d0, d2 = a + b, a - b
                result.append(
                    (
                        after,
                        red + weight * pl.reciprocal(d0, approx=True),
                        green + weight * pl.reciprocal(d1, approx=True),
                        blue + weight * pl.reciprocal(d2, approx=True),
                    )
                )
            return result

        groups = [tuple(c[r : r + TILE] for c in carry) for r in starts]
        for lo, hi, whole in segments(x_lo, x_hi, SHEAR_Y[v], layers):

            def body(xs, inner, whole=whole):
                for x in xs:
                    inner = layer(x, whole, inner)
                return inner

            groups = blocked(lo, hi, STEP, body, groups)
        return tuple(jnp.concatenate([g[c] for g in groups], axis=0) for c in range(4))

    zero = jnp.zeros((half, cols), jnp.float32)
    one = jnp.ones((half, cols), jnp.float32)

    start_carry = (one, zero, zero, zero)
    order = [0, VIEWS - 1] + list(range(1, VIEWS - 1))
    units = [(v, h) for v in order for h in range(2)]
    for place in range(EARLY):
        v, h = units[place]
        inner = render(v, h * half, halo, layers - halo, start_carry)
        for c in range(4):
            stash[place, c] = inner[c]

    arrive(edge_copies)
    start(corner_copies)
    arrive(mid_copies)
    arrive(corner_copies)
    for k in range(SWEEPS):
        sweep(k, stages[k], stages[k + 1], 1 + k, halo + 1 + k, True)
        sweep(k, stages[k], stages[k + 1], halo + layers - 1 - k, total - 1 - k, True)

    outs = [
        pltpu.make_async_copy(
            u3.at[f, pl.ds(halo, layers), pl.ds(TILE, rows), :],
            (phase_out, heat_out)[f],
            out_sem.at[f],
        )
        for f in range(2)
    ]
    for copy in outs:
        copy.start()

    def piece_of(place):
        v, h = units[place]
        if place < EARLY:
            trans, *colours = render(v, h * half, 0, halo, start_carry)
            inner = [stash[place, c] for c in range(4)]
            carry = (trans * inner[0],) + tuple(
                colours[c] + trans * inner[1 + c] for c in range(3)
            )
            carry = render(v, h * half, layers - halo, layers, carry)
        else:
            carry = render(v, h * half, 0, layers, start_carry)
        trans, red, green, blue = carry
        return [red, green, blue, trans]

    if not swap:
        for place, (v, h) in enumerate(units):
            part = piece_of(place)
            for c in range(4):
                picture_ref[c, h * half : (h + 1) * half, v * cols : (v + 1) * cols] = part[c]
    else:
        quarter = half // 2
        left_lanes = lax.broadcasted_iota(jnp.int32, (quarter, cols), 1) < cols // 2

        def pair_copy(v, h):
            return pltpu.make_async_remote_copy(
                src_ref=sent.at[v, h],
                dst_ref=xrecv.at[v, h],
                send_sem=ps_sem.at[v, h],
                recv_sem=pr_sem.at[v, h],
                device_id=(partner, l),
                device_id_type=MESH,
            )

        def group_copy(v, h, slot):
            return pltpu.make_async_remote_copy(
                src_ref=merged.at[v, h],
                dst_ref=zrecv.at[slot, h],
                send_sem=zs_sem.at[v, h],
                recv_sem=zr_sem.at[slot, h],
                device_id=(2 * v + xbit, l),
                device_id_type=MESH,
            )

        def send_pair(place):
            v, h = units[place]
            part = piece_of(place)
            for c in range(4):
                lo, hi = part[c][:quarter], part[c][quarter:]
                lower = jnp.where(left_lanes, lo, pltpu.roll(hi, cols // 2, 1))
                upper = jnp.where(left_lanes, pltpu.roll(lo, cols // 2, 1), hi)
                keep[v, h, c] = jnp.where(xbit == 0, lower, upper)
                sent[v, h, c] = jnp.where(xbit == 0, upper, lower)
            pair_copy(v, h).start()

        def send_group(place):
            v, h = units[place]
            pair_copy(v, h).wait_recv()
            mine = [keep[v, h, c] for c in range(4)]
            other = [xrecv[v, h, c] for c in range(4)]
            front = [jnp.where(xbit == 0, m, o) for m, o in zip(mine, other)]
            behind = [jnp.where(xbit == 0, o, m) for m, o in zip(mine, other)]
            result = over(front, behind)

            @pl.when(myz == v)
            def _():
                for c in range(4):
                    zrecv[v, h, c] = result[c]

            @pl.when(myz != v)
            def _():
                for c in range(4):
                    merged[v, h, c] = result[c]
                group_copy(v, h, myz).start()

        for place in range(len(units)):
            send_pair(place)
            if place >= 2:
                send_group(place - 2)
        send_group(len(units) - 2)
        send_group(len(units) - 1)

        for h in range(2):
            for s in range(VIEWS):
                pl.when(myz != s)(group_copy(s, h, s).wait_recv)
            result = [zrecv[VIEWS - 1, h, c] for c in range(4)]
            for s in range(VIEWS - 2, -1, -1):
                result = over([zrecv[s, h, c] for c in range(4)], result)
            for c in range(4):
                picture_ref[h, c] = result[c]
        for v, h in units:
            pair_copy(v, h).wait_send()
            pl.when(myz != v)(group_copy(v, h, myz).wait_send)

    for entries in lat_copies:
        leave(entries)
    leave(edge_copies)
    leave(mid_copies)
    leave(corner_copies)
    for copy in outs:
        copy.wait()


def deliver(phase_ref, heat_ref, packed_ref, phase_out, heat_out, picture_ref, held, into, out):
    layers = phase_ref.shape[0]
    size = layers // CHUNKS
    pairs = ((phase_ref, phase_out), (heat_ref, heat_out))
    arrivals, departures = [], []
    for f, (source, target) in enumerate(pairs):
        for n in range(CHUNKS):
            part = pl.ds(n * size, size)
            arrivals.append(
                pltpu.make_async_copy(source.at[part], held.at[f, part], into.at[f, n])
            )
            departures.append(
                pltpu.make_async_copy(held.at[f, part], target.at[part], out.at[f, n])
            )
    for copy in arrivals:
        copy.start()
    halves, channels, quarter, cols = packed_ref.shape
    for h in range(halves):
        for c in range(channels):
            part = packed_ref[h, c]
            first = 2 * h * quarter
            picture_ref[c, first : first + quarter, :] = part[:, : cols // 2]
            picture_ref[c, first + quarter : first + 2 * quarter, :] = pltpu.roll(
                part, cols // 2, 1
            )[:, : cols // 2]
    for arrival, departure in zip(arrivals, departures):
        arrival.wait()
        departure.start()
    for copy in departures:
        copy.wait()


def from_partner(shard, axis, apart):
    return lax.ppermute(shard, axis, [(i, i ^ 1 << apart) for i in range(lax.axis_size(axis))])


def over_blend(in_front, behind):
    return jnp.concatenate(
        [in_front[:3] + in_front[3:] * behind[:3], in_front[3:] * behind[3:]], axis=0
    )


def binary_swap(picture, depth_size):
    row_count, pixels = picture.shape[1:]
    bit_count = depth_size.bit_length() - 1
    block_width = pixels >> bit_count
    shaped = picture.reshape((4, row_count) + (2,) * bit_count + (block_width,))
    permuted = (0, 1) + tuple(range(bit_count + 1, 1, -1)) + (bit_count + 2,)
    picture = jnp.transpose(shaped, permuted).reshape(4, row_count, pixels)
    my_index = lax.axis_index("depth")
    for b in range(bit_count):
        half_width = picture.shape[2] // 2
        front_half = picture[:, :, :half_width]
        second = picture[:, :, half_width:]
        upper_bit = my_index >> b & 1 == 1
        kept_half = jnp.where(upper_bit, second, front_half)
        sent_half = jnp.where(upper_bit, front_half, second)
        partner = from_partner(sent_half, "depth", b)
        in_front = jnp.where(upper_bit, partner, kept_half)
        behind = jnp.where(upper_bit, kept_half, partner)
        picture = over_blend(in_front, behind)
    return picture


def per_device(phase, temper, iface_count):
    layers, rows, cols = phase.shape
    depth_size = lax.axis_size("depth")
    lat_size = lax.axis_size("lat")
    swap = depth_size == 2 * VIEWS
    packed = (2, 4, rows // 4, cols)
    piece = packed if swap else (4, rows, VIEWS * cols)
    grid = (2, layers + 2 * SWEEPS, rows + 2 * TILE, cols)
    tile = (VIEWS,) + packed
    dma = pltpu.SemaphoreType.DMA
    phase_next, heat_next, picture = pl.pallas_call(
        functools.partial(kernel, depth_size, lat_size, swap),
        out_shape=(
            jax.ShapeDtypeStruct(phase.shape, jnp.float32),
            jax.ShapeDtypeStruct(phase.shape, jnp.float32),
            jax.ShapeDtypeStruct(piece, jnp.float32),
        ),
        in_specs=[
            pl.BlockSpec(memory_space=pl.ANY),
            pl.BlockSpec(memory_space=pl.ANY),
            pl.BlockSpec(memory_space=pltpu.SMEM),
        ],
        out_specs=(
            pl.BlockSpec(memory_space=pl.ANY),
            pl.BlockSpec(memory_space=pl.ANY),
            pl.BlockSpec(memory_space=pltpu.VMEM),
        ),
        scratch_shapes=[pltpu.VMEM(grid, jnp.float32) for _ in range(5)]
        + [pltpu.VMEM((EARLY, 4, rows // 2, cols), jnp.float32)]
        + [pltpu.VMEM(tile, jnp.float32) for _ in range(5)]
        + [
            dma((2,)),
            dma((2,)),
            dma((3, 2, 2)),
            dma((3, 2, 2)),
            dma((GROUPS, 2, 2)),
            dma((GROUPS, 2, 2)),
            dma((2, 2)),
            dma((2, 2)),
            dma((VIEWS, 2)),
            dma((VIEWS, 2)),
            dma((VIEWS, 2)),
            dma((VIEWS, 2)),
        ],
        compiler_params=pltpu.CompilerParams(
            collective_id=0, has_side_effects=True, vmem_limit_bytes=60 * 1024 * 1024
        ),
    )(phase, temper, iface_count)
    if not swap:
        return phase_next, heat_next, binary_swap(picture, depth_size)
    return pl.pallas_call(
        deliver,
        out_shape=(
            jax.ShapeDtypeStruct(phase.shape, jnp.float32),
            jax.ShapeDtypeStruct(phase.shape, jnp.float32),
            jax.ShapeDtypeStruct((4, rows, cols // 2), jnp.float32),
        ),
        in_specs=[
            pl.BlockSpec(memory_space=pl.ANY),
            pl.BlockSpec(memory_space=pl.ANY),
            pl.BlockSpec(memory_space=pltpu.VMEM),
        ],
        out_specs=(
            pl.BlockSpec(memory_space=pl.ANY),
            pl.BlockSpec(memory_space=pl.ANY),
            pl.BlockSpec(memory_space=pltpu.VMEM),
        ),
        scratch_shapes=[
            pltpu.VMEM((2,) + phase.shape, jnp.float32),
            dma((2, CHUNKS)),
            dma((2, CHUNKS)),
        ],
        compiler_params=pltpu.CompilerParams(vmem_limit_bytes=60 * 1024 * 1024),
    )(phase_next, heat_next, picture)


def solution(mesh):
    return jax.shard_map(
        per_device,
        mesh=mesh,
        in_specs=(P("depth", "lat", None), P("depth", "lat", None), P("depth", "lat")),
        out_specs=(P("depth", "lat", None), P("depth", "lat", None), P(None, "lat", "depth")),
        check_vma=False,
    )
```

```python
import functools
import math

import jax
import jax.numpy as jnp
import numpy as np
from jax import lax
from jax.experimental import pallas as pl
from jax.experimental.pallas import tpu as pltpu
from jax.sharding import PartitionSpec as P

SWEEPS = 3

DIFFUSION = (0.5, 2.0)
TIME_STEP = 0.4
COUPLE = 0.6
LATENT = 0.5
SHEAR_Y = (1.6, -1.6, 0.8, -1.2)
SHEAR_Z = (0.9, -0.6, -0.9, 0.3)
CENTERS = (-0.8, 0.0, 0.8)
VIEWS = len(SHEAR_Y)
MESH = pl.DeviceIdType.MESH
TILE = 8
REACH = 4
GROUPS = 4
WINDOW = 4
CHUNKS = 8
STEP = 8
EARLY = 1


def thetas(sweep_total):
    chebyshev = []
    for f in range(2):
        highest = 1.0 + 12.0 * DIFFUSION[f]
        entries = [
            0.5 * (highest + 1.0)
            + 0.5 * (highest - 1.0) * math.cos((2 * j + 1) * math.pi / (2 * sweep_total))
            for j in range(sweep_total)
        ]
        chebyshev.append(entries)
    return np.array(chebyshev)


def over(front, behind):
    return [front[c] + front[3] * behind[c] for c in range(3)] + [front[3] * behind[3]]


def segments(x_lo, x_hi, shear, layers):
    runs = []
    for x in range(x_lo, x_hi):
        whole = int(math.floor(abs(shear) * x / layers))
        if runs and runs[-1][2] == whole:
            runs[-1][1] = x + 1
        else:
            runs.append([x, x + 1, whole])
    return runs


def blocked(lo, hi, step, body, carry):
    count = (hi - lo) // step

    def block(i, inner):
        return body([lo + i * step + j for j in range(step)], inner)

    if count:
        carry = lax.fori_loop(0, count, block, carry)
    rest = list(range(lo + count * step, hi))
    return body(rest, carry) if rest else carry


def kernel(
    depth_size,
    lat_size,
    swap,
    phase_ref,
    temper_ref,
    count_ref,
    phase_out,
    heat_out,
    picture_ref,
    u0,
    u1,
    u2,
    u3,
    src,
    stash,
    keep,
    sent,
    xrecv,
    merged,
    zrecv,
    in_sem,
    out_sem,
    xs_sem,
    xr_sem,
    ys_sem,
    yr_sem,
    cs_sem,
    cr_sem,
    ps_sem,
    pr_sem,
    zs_sem,
    zr_sem,
):
    layers, rows, cols = phase_ref.shape
    halo = SWEEPS
    d = lax.axis_index("depth")
    l = lax.axis_index("lat")
    has_prev, has_next = d > 0, d < depth_size - 1
    has_low, has_high = l > 0, l < lat_size - 1
    up, down = lax.rem(d + 1, depth_size), lax.rem(d + depth_size - 1, depth_size)
    right, left = lax.rem(l + 1, lat_size), lax.rem(l + lat_size - 1, lat_size)
    xbit = lax.rem(d, 2)
    myz = d // 2
    partner = d + 1 - 2 * xbit
    fields = (phase_ref, temper_ref)

    local = [
        pltpu.make_async_copy(
            fields[f], u0.at[f, pl.ds(halo, layers), pl.ds(TILE, rows), :], in_sem.at[f]
        )
        for f in range(2)
    ]
    for copy in local:
        copy.start()

    barrier = pltpu.get_barrier_semaphore()
    greet = ((has_prev, (down, l)), (has_next, (up, l)), (has_low, (d, left)), (has_high, (d, right)))
    for there, device in greet:

        @pl.when(there)
        def _():
            pl.semaphore_signal(barrier, inc=1, device_id=device, device_id_type=MESH)

    if swap:
        for z in range(VIEWS):

            @pl.when(myz != z)
            def _():
                pl.semaphore_signal(
                    barrier, inc=1, device_id=(2 * z + xbit, l), device_id_type=MESH
                )

    @pl.when(d == 0)
    def _():
        u0[:, :halo] = jnp.zeros((2, halo, rows + 2 * TILE, cols), jnp.float32)

    @pl.when(d == depth_size - 1)
    def _():
        u0[:, halo + layers :] = jnp.zeros((2, halo, rows + 2 * TILE, cols), jnp.float32)

    for edge, first in ((l == 0, 0), (l == lat_size - 1, TILE + rows)):

        @pl.when(edge)
        def _():
            def clear(x, carry):
                for f in range(2):
                    u0[f, x, pl.ds(first, TILE), :] = jnp.zeros((TILE, cols), jnp.float32)
                return carry

            lax.fori_loop(0, layers + 2 * halo, clear, 0)

    peers = sum(
        jnp.minimum(n, 1) for n in (d, depth_size - 1 - d, l, lat_size - 1 - l)
    )
    pl.semaphore_wait(barrier, peers + (VIEWS - 1 if swap else 0))

    lat_copies, edge_copies, mid_copies, corner_copies = [], [], [], []
    groups = GROUPS if layers % GROUPS == 0 else 1
    depth = layers // groups
    for g in range(groups):
        lat_copies.append([])
        for way in range(2):
            row_from, row_to = ((rows - TILE, 0), (0, TILE + rows))[way]
            for f in range(2):
                copy = pltpu.make_async_remote_copy(
                    src_ref=fields[f].at[pl.ds(g * depth, depth), pl.ds(row_from, TILE), :],
                    dst_ref=u0.at[f, pl.ds(halo + g * depth, depth), pl.ds(row_to, TILE), :],
                    send_sem=ys_sem.at[g, way, f],
                    recv_sem=yr_sem.at[g, way, f],
                    device_id=(d, (right, left)[way]),
                    device_id_type=MESH,
                )
                entry = ((has_high, has_low)[way], (has_low, has_high)[way], copy)
                lat_copies[g].append(entry)
    pieces = ((0, TILE), (rows - TILE, TILE), (TILE, rows - 2 * TILE))
    for piece, (row, size) in enumerate(pieces):
        for way in range(2):
            layer_from, layer_to = ((layers - halo, 0), (0, halo + layers))[way]
            for f in range(2):
                copy = pltpu.make_async_remote_copy(
                    src_ref=fields[f].at[pl.ds(layer_from, halo), pl.ds(row, size), :],
                    dst_ref=u0.at[f, pl.ds(layer_to, halo), pl.ds(TILE + row, size), :],
                    send_sem=xs_sem.at[piece, way, f],
                    recv_sem=xr_sem.at[piece, way, f],
                    device_id=((up, down)[way], l),
                    device_id_type=MESH,
                )
                entry = ((has_next, has_prev)[way], (has_prev, has_next)[way], copy)
                (mid_copies if piece == 2 else edge_copies).append(entry)
    for side in range(2):
        layer = (0, halo + layers)[side]
        filled = (has_prev, has_next)[side]
        for way in range(2):
            row_from, row_to = ((rows, 0), (TILE, TILE + rows))[way]
            copy = pltpu.make_async_remote_copy(
                src_ref=u0.at[:, pl.ds(layer, halo), pl.ds(row_from, TILE), :],
                dst_ref=u0.at[:, pl.ds(layer, halo), pl.ds(row_to, TILE), :],
                send_sem=cs_sem.at[side, way],
                recv_sem=cr_sem.at[side, way],
                device_id=(d, (right, left)[way]),
                device_id_type=MESH,
            )
            sends = jnp.logical_and(filled, (has_high, has_low)[way])
            receives = jnp.logical_and(filled, (has_low, has_high)[way])
            corner_copies.append((sends, receives, copy))

    def start(entries):
        for sends, _receives, copy in entries:
            pl.when(sends)(copy.start)

    def arrive(entries):
        for _sends, receives, copy in entries:
            pl.when(receives)(copy.wait_recv)

    def leave(entries):
        for sends, _receives, copy in entries:
            pl.when(sends)(copy.wait_send)

    start(edge_copies)
    start(lat_copies[0])
    start(mid_copies)
    for g in range(1, groups):
        start(lat_copies[g])
    for copy in local:
        copy.wait()

    chebyshev = thetas(SWEEPS)
    first_row = TILE - REACH
    span = rows + 2 * REACH
    chunk = next(n for n in (24, 16, 8) if span % n == 0)
    lane = lax.broadcasted_iota(jnp.int32, (chunk, cols), 1)
    row_id = lax.broadcasted_iota(jnp.int32, (chunk, cols), 0)
    low_mask = jnp.where(jnp.logical_or(row_id >= REACH, has_low), 1.0, 0.0)
    high_mask = jnp.where(jnp.logical_or(row_id < chunk - REACH, has_high), 1.0, 0.0)

    def sweep(k, before, after, x_lo, x_hi, edge):
        def body(xs, carry):
            for x in xs:
                factor = None
                if edge:
                    inside = jnp.logical_and(
                        jnp.logical_or(x >= halo, has_prev),
                        jnp.logical_or(x < halo + layers, has_next),
                    )
                    factor = jnp.where(inside, 1.0, 0.0)
                for r0 in range(first_row, first_row + span, chunk):
                    here = pl.ds(r0, chunk)
                    values = [before[f, x, here, :] for f in range(2)]
                    if k == 0:
                        p, t = values
                        reaction = p * (1.0 - p) * (p - 0.5 + COUPLE * t)
                        sources = [p + TIME_STEP * reaction, t + LATENT * TIME_STEP * reaction]
                    else:
                        sources = [src[f, x, here, :] for f in range(2)]
                    for f in range(2):
                        u = values[f]
                        around = before[f, x - 1, here, :] + before[f, x + 1, here, :]
                        around = around + (
                            before[f, x, pl.ds(r0 - 1, chunk), :]
                            + before[f, x, pl.ds(r0 + 1, chunk), :]
                        )
                        around = around + (
                            jnp.where(lane == 0, 0.0, pltpu.roll(u, 1, 1))
                            + jnp.where(lane == cols - 1, 0.0, pltpu.roll(u, cols - 1, 1))
                        )
                        theta = chebyshev[f, k]
                        new = (
                            float(1.0 - (1.0 + 6.0 * DIFFUSION[f]) / theta) * u
                            + float(1.0 / theta) * sources[f]
                            + float(DIFFUSION[f] / theta) * around
                        )
                        if r0 == first_row:
                            new = new * low_mask
                        if r0 + chunk == first_row + span:
                            new = new * high_mask
                        if edge:
                            new = new * factor
                        after[f, x, here, :] = new
                        if k == 0:
                            src[f, x, here, :] = sources[f]
            return carry

        blocked(x_lo, x_hi, 4, body, 0)

    stages = (u0, u1, u2, u3)
    total = layers + 2 * halo
    ready = halo + 1
    for g in range(groups):
        arrive(lat_copies[g])
        until = halo + (g + 1) * depth - 1
        sweep(0, u0, u1, ready, until, False)
        ready = until
    for k in range(1, SWEEPS):
        sweep(k, stages[k], stages[k + 1], halo + 1 + k, halo + layers - 1 - k, False)

    half = rows // 2
    count = count_ref[0, 0]
    lane1 = lax.broadcasted_iota(jnp.int32, (TILE, cols), 1)
    first_lane, last_lane = lane1 == 0, lane1 == cols - 1
    opacity = 4.0 / (layers * depth_size)
    starts = range(0, half, TILE)

    def render(v, r0, x_lo, x_hi, carry):
        sy = 1 if SHEAR_Y[v] > 0 else -1
        sz = 1 if SHEAR_Z[v] > 0 else -1
        edge_lane = last_lane if sz > 0 else first_lane

        def layer(x, whole, groups):
            xf = lax.convert_element_type(x, jnp.float32)
            fy = xf * (abs(SHEAR_Y[v]) / layers) - whole
            fz = xf * (abs(SHEAR_Z[v]) / layers)
            far_z = jnp.where(edge_lane, 0.0, fz)
            near_z = 1.0 - fz
            scale = jnp.where(x < count, -opacity, 0.0)
            result = []
            for row, (trans, red, green, blue) in zip(starts, groups):
                sampled = []
                for f in range(2):
                    first = TILE + r0 + row
                    near = u3[f, x + halo, pl.ds(first + sy * whole, TILE), :]
                    far = u3[f, x + halo, pl.ds(first + sy * (whole + 1), TILE), :]
                    b = near + fy * (far - near)
                    beside = pltpu.roll(b, cols - 1 if sz > 0 else 1, 1)
                    sampled.append(near_z * b + far_z * beside)
                after = trans * jnp.exp(scale * (sampled[0] * sampled[0]))
                weight = trans - after
                s = sampled[1]
                q = s * s
                d1 = q + 1.0
                a = q + (1.0 + CENTERS[2] * CENTERS[2])
                b = (2.0 * CENTERS[2]) * s
                d0, d2 = a + b, a - b
                result.append(
                    (
                        after,
                        red + weight * pl.reciprocal(d0, approx=True),
                        green + weight * pl.reciprocal(d1, approx=True),
                        blue + weight * pl.reciprocal(d2, approx=True),
                    )
                )
            return result

        groups = [tuple(c[r : r + TILE] for c in carry) for r in starts]
        for lo, hi, whole in segments(x_lo, x_hi, SHEAR_Y[v], layers):

            def body(xs, inner, whole=whole):
                for x in xs:
                    inner = layer(x, whole, inner)
                return inner

            groups = blocked(lo, hi, STEP, body, groups)
        return tuple(jnp.concatenate([g[c] for g in groups], axis=0) for c in range(4))

    zero = jnp.zeros((half, cols), jnp.float32)
    one = jnp.ones((half, cols), jnp.float32)

    start_carry = (one, zero, zero, zero)
    order = [0, VIEWS - 1] + list(range(1, VIEWS - 1))
    units = [(v, h) for v in order for h in range(2)]
    for place in range(EARLY):
        v, h = units[place]
        inner = render(v, h * half, halo, layers - halo, start_carry)
        for c in range(4):
            stash[place, c] = inner[c]

    arrive(edge_copies)
    start(corner_copies)
    arrive(mid_copies)
    arrive(corner_copies)
    for k in range(SWEEPS):
        sweep(k, stages[k], stages[k + 1], 1 + k, halo + 1 + k, True)
        sweep(k, stages[k], stages[k + 1], halo + layers - 1 - k, total - 1 - k, True)

    outs = [
        pltpu.make_async_copy(
            u3.at[f, pl.ds(halo, layers), pl.ds(TILE, rows), :],
            (phase_out, heat_out)[f],
            out_sem.at[f],
        )
        for f in range(2)
    ]
    for copy in outs:
        copy.start()

    def piece_of(place):
        v, h = units[place]
        if place < EARLY:
            trans, *colours = render(v, h * half, 0, halo, start_carry)
            inner = [stash[place, c] for c in range(4)]
            carry = (trans * inner[0],) + tuple(
                colours[c] + trans * inner[1 + c] for c in range(3)
            )
            carry = render(v, h * half, layers - halo, layers, carry)
        else:
            carry = render(v, h * half, 0, layers, start_carry)
        trans, red, green, blue = carry
        return [red, green, blue, trans]

    if not swap:
        for place, (v, h) in enumerate(units):
            part = piece_of(place)
            for c in range(4):
                picture_ref[c, h * half : (h + 1) * half, v * cols : (v + 1) * cols] = part[c]
    else:
        quarter = half // 2
        left_lanes = lax.broadcasted_iota(jnp.int32, (quarter, cols), 1) < cols // 2

        def pair_copy(v, h):
            return pltpu.make_async_remote_copy(
                src_ref=sent.at[v, h],
                dst_ref=xrecv.at[v, h],
                send_sem=ps_sem.at[v, h],
                recv_sem=pr_sem.at[v, h],
                device_id=(partner, l),
                device_id_type=MESH,
            )

        def group_copy(v, h, slot):
            return pltpu.make_async_remote_copy(
                src_ref=merged.at[v, h],
                dst_ref=zrecv.at[slot, h],
                send_sem=zs_sem.at[v, h],
                recv_sem=zr_sem.at[slot, h],
                device_id=(2 * v + xbit, l),
                device_id_type=MESH,
            )

        def send_pair(place):
            v, h = units[place]
            part = piece_of(place)
            for c in range(4):
                lo, hi = part[c][:quarter], part[c][quarter:]
                lower = jnp.where(left_lanes, lo, pltpu.roll(hi, cols // 2, 1))
                upper = jnp.where(left_lanes, pltpu.roll(lo, cols // 2, 1), hi)
                keep[v, h, c] = jnp.where(xbit == 0, lower, upper)
                sent[v, h, c] = jnp.where(xbit == 0, upper, lower)
            pair_copy(v, h).start()

        def send_group(place):
            v, h = units[place]
            pair_copy(v, h).wait_recv()
            mine = [keep[v, h, c] for c in range(4)]
            other = [xrecv[v, h, c] for c in range(4)]
            front = [jnp.where(xbit == 0, m, o) for m, o in zip(mine, other)]
            behind = [jnp.where(xbit == 0, o, m) for m, o in zip(mine, other)]
            result = over(front, behind)

            @pl.when(myz == v)
            def _():
                for c in range(4):
                    zrecv[v, h, c] = result[c]

            @pl.when(myz != v)
            def _():
                for c in range(4):
                    merged[v, h, c] = result[c]
                group_copy(v, h, myz).start()

        for place in range(len(units)):
            send_pair(place)
            if place >= 2:
                send_group(place - 2)
        send_group(len(units) - 2)
        send_group(len(units) - 1)

        for h in range(2):
            for s in range(VIEWS):
                pl.when(myz != s)(group_copy(s, h, s).wait_recv)
            result = [zrecv[VIEWS - 1, h, c] for c in range(4)]
            for s in range(VIEWS - 2, -1, -1):
                result = over([zrecv[s, h, c] for c in range(4)], result)
            for c in range(4):
                picture_ref[h, c] = result[c]
        for v, h in units:
            pair_copy(v, h).wait_send()
            pl.when(myz != v)(group_copy(v, h, myz).wait_send)

    for entries in lat_copies:
        leave(entries)
    leave(edge_copies)
    leave(mid_copies)
    leave(corner_copies)
    for copy in outs:
        copy.wait()


def deliver(phase_ref, heat_ref, packed_ref, phase_out, heat_out, picture_ref, held, into, out):
    layers = phase_ref.shape[0]
    size = layers // CHUNKS
    pairs = ((phase_ref, phase_out), (heat_ref, heat_out))
    arrivals, departures = [], []
    for f, (source, target) in enumerate(pairs):
        for n in range(CHUNKS):
            part = pl.ds(n * size, size)
            arrivals.append(
                pltpu.make_async_copy(source.at[part], held.at[f, part], into.at[f, n])
            )
            departures.append(
                pltpu.make_async_copy(held.at[f, part], target.at[part], out.at[f, n])
            )
    for copy in arrivals[:WINDOW]:
        copy.start()
    halves, channels, quarter, cols = packed_ref.shape
    for h in range(halves):
        for c in range(channels):
            part = packed_ref[h, c]
            first = 2 * h * quarter
            picture_ref[c, first : first + quarter, :] = part[:, : cols // 2]
            picture_ref[c, first + quarter : first + 2 * quarter, :] = pltpu.roll(
                part, cols // 2, 1
            )[:, : cols // 2]
    for n, (arrival, departure) in enumerate(zip(arrivals, departures)):
        arrival.wait()
        departure.start()
        if n + WINDOW < len(arrivals):
            arrivals[n + WINDOW].start()
    for copy in departures:
        copy.wait()


def from_partner(shard, axis, apart):
    return lax.ppermute(shard, axis, [(i, i ^ 1 << apart) for i in range(lax.axis_size(axis))])


def over_blend(in_front, behind):
    return jnp.concatenate(
        [in_front[:3] + in_front[3:] * behind[:3], in_front[3:] * behind[3:]], axis=0
    )


def binary_swap(picture, depth_size):
    row_count, pixels = picture.shape[1:]
    bit_count = depth_size.bit_length() - 1
    block_width = pixels >> bit_count
    shaped = picture.reshape((4, row_count) + (2,) * bit_count + (block_width,))
    permuted = (0, 1) + tuple(range(bit_count + 1, 1, -1)) + (bit_count + 2,)
    picture = jnp.transpose(shaped, permuted).reshape(4, row_count, pixels)
    my_index = lax.axis_index("depth")
    for b in range(bit_count):
        half_width = picture.shape[2] // 2
        front_half = picture[:, :, :half_width]
        second = picture[:, :, half_width:]
        upper_bit = my_index >> b & 1 == 1
        kept_half = jnp.where(upper_bit, second, front_half)
        sent_half = jnp.where(upper_bit, front_half, second)
        partner = from_partner(sent_half, "depth", b)
        in_front = jnp.where(upper_bit, partner, kept_half)
        behind = jnp.where(upper_bit, kept_half, partner)
        picture = over_blend(in_front, behind)
    return picture


def per_device(phase, temper, iface_count):
    layers, rows, cols = phase.shape
    depth_size = lax.axis_size("depth")
    lat_size = lax.axis_size("lat")
    swap = depth_size == 2 * VIEWS
    packed = (2, 4, rows // 4, cols)
    piece = packed if swap else (4, rows, VIEWS * cols)
    grid = (2, layers + 2 * SWEEPS, rows + 2 * TILE, cols)
    tile = (VIEWS,) + packed
    dma = pltpu.SemaphoreType.DMA
    phase_next, heat_next, picture = pl.pallas_call(
        functools.partial(kernel, depth_size, lat_size, swap),
        out_shape=(
            jax.ShapeDtypeStruct(phase.shape, jnp.float32),
            jax.ShapeDtypeStruct(phase.shape, jnp.float32),
            jax.ShapeDtypeStruct(piece, jnp.float32),
        ),
        in_specs=[
            pl.BlockSpec(memory_space=pl.ANY),
            pl.BlockSpec(memory_space=pl.ANY),
            pl.BlockSpec(memory_space=pltpu.SMEM),
        ],
        out_specs=(
            pl.BlockSpec(memory_space=pl.ANY),
            pl.BlockSpec(memory_space=pl.ANY),
            pl.BlockSpec(memory_space=pltpu.VMEM),
        ),
        scratch_shapes=[pltpu.VMEM(grid, jnp.float32) for _ in range(5)]
        + [pltpu.VMEM((EARLY, 4, rows // 2, cols), jnp.float32)]
        + [pltpu.VMEM(tile, jnp.float32) for _ in range(5)]
        + [
            dma((2,)),
            dma((2,)),
            dma((3, 2, 2)),
            dma((3, 2, 2)),
            dma((GROUPS, 2, 2)),
            dma((GROUPS, 2, 2)),
            dma((2, 2)),
            dma((2, 2)),
            dma((VIEWS, 2)),
            dma((VIEWS, 2)),
            dma((VIEWS, 2)),
            dma((VIEWS, 2)),
        ],
        compiler_params=pltpu.CompilerParams(
            collective_id=0, has_side_effects=True, vmem_limit_bytes=60 * 1024 * 1024
        ),
    )(phase, temper, iface_count)
    if not swap:
        return phase_next, heat_next, binary_swap(picture, depth_size)
    return pl.pallas_call(
        deliver,
        out_shape=(
            jax.ShapeDtypeStruct(phase.shape, jnp.float32),
            jax.ShapeDtypeStruct(phase.shape, jnp.float32),
            jax.ShapeDtypeStruct((4, rows, cols // 2), jnp.float32),
        ),
        in_specs=[
            pl.BlockSpec(memory_space=pl.ANY),
            pl.BlockSpec(memory_space=pl.ANY),
            pl.BlockSpec(memory_space=pltpu.VMEM),
        ],
        out_specs=(
            pl.BlockSpec(memory_space=pl.ANY),
            pl.BlockSpec(memory_space=pl.ANY),
            pl.BlockSpec(memory_space=pltpu.VMEM),
        ),
        scratch_shapes=[
            pltpu.VMEM((2,) + phase.shape, jnp.float32),
            dma((2, CHUNKS)),
            dma((2, CHUNKS)),
        ],
        compiler_params=pltpu.CompilerParams(vmem_limit_bytes=60 * 1024 * 1024),
    )(phase_next, heat_next, picture)


def solution(mesh):
    return jax.shard_map(
        per_device,
        mesh=mesh,
        in_specs=(P("depth", "lat", None), P("depth", "lat", None), P("depth", "lat")),
        out_specs=(P("depth", "lat", None), P("depth", "lat", None), P(None, "lat", "depth")),
        check_vma=False,
    )
```

```python
import functools
import math

import jax
import jax.numpy as jnp
import numpy as np
from jax import lax
from jax.experimental import pallas as pl
from jax.experimental.pallas import tpu as pltpu
from jax.sharding import PartitionSpec as P

SWEEPS = 3

DIFFUSION = (0.5, 2.0)
TIME_STEP = 0.4
COUPLE = 0.6
LATENT = 0.5
SHEAR_Y = (1.6, -1.6, 0.8, -1.2)
SHEAR_Z = (0.9, -0.6, -0.9, 0.3)
CENTERS = (-0.8, 0.0, 0.8)
VIEWS = len(SHEAR_Y)
MESH = pl.DeviceIdType.MESH
TILE = 8
REACH = 4
GROUPS = 4
CHUNKS = 4
STEP = 8
EARLY = 1


def thetas(sweep_total):
    chebyshev = []
    for f in range(2):
        highest = 1.0 + 12.0 * DIFFUSION[f]
        entries = [
            0.5 * (highest + 1.0)
            + 0.5 * (highest - 1.0) * math.cos((2 * j + 1) * math.pi / (2 * sweep_total))
            for j in range(sweep_total)
        ]
        chebyshev.append(entries)
    return np.array(chebyshev)


def over(front, behind):
    return [front[c] + front[3] * behind[c] for c in range(3)] + [front[3] * behind[3]]


def segments(x_lo, x_hi, shear, layers):
    runs = []
    for x in range(x_lo, x_hi):
        whole = int(math.floor(abs(shear) * x / layers))
        if runs and runs[-1][2] == whole:
            runs[-1][1] = x + 1
        else:
            runs.append([x, x + 1, whole])
    return runs


def blocked(lo, hi, step, body, carry):
    count = (hi - lo) // step

    def block(i, inner):
        return body([lo + i * step + j for j in range(step)], inner)

    if count:
        carry = lax.fori_loop(0, count, block, carry)
    rest = list(range(lo + count * step, hi))
    return body(rest, carry) if rest else carry


def kernel(
    depth_size,
    lat_size,
    swap,
    phase_ref,
    temper_ref,
    count_ref,
    phase_out,
    heat_out,
    picture_ref,
    u0,
    u1,
    u2,
    u3,
    src,
    stash,
    keep,
    sent,
    xrecv,
    merged,
    zrecv,
    in_sem,
    out_sem,
    xs_sem,
    xr_sem,
    ys_sem,
    yr_sem,
    cs_sem,
    cr_sem,
    ps_sem,
    pr_sem,
    zs_sem,
    zr_sem,
):
    layers, rows, cols = phase_ref.shape
    halo = SWEEPS
    d = lax.axis_index("depth")
    l = lax.axis_index("lat")
    has_prev, has_next = d > 0, d < depth_size - 1
    has_low, has_high = l > 0, l < lat_size - 1
    up, down = lax.rem(d + 1, depth_size), lax.rem(d + depth_size - 1, depth_size)
    right, left = lax.rem(l + 1, lat_size), lax.rem(l + lat_size - 1, lat_size)
    xbit = lax.rem(d, 2)
    myz = d // 2
    partner = d + 1 - 2 * xbit
    fields = (phase_ref, temper_ref)

    local = [
        pltpu.make_async_copy(
            fields[f], u0.at[f, pl.ds(halo, layers), pl.ds(TILE, rows), :], in_sem.at[f]
        )
        for f in range(2)
    ]
    for copy in local:
        copy.start()

    barrier = pltpu.get_barrier_semaphore()
    greet = ((has_prev, (down, l)), (has_next, (up, l)), (has_low, (d, left)), (has_high, (d, right)))
    for there, device in greet:

        @pl.when(there)
        def _():
            pl.semaphore_signal(barrier, inc=1, device_id=device, device_id_type=MESH)

    if swap:
        for z in range(VIEWS):

            @pl.when(myz != z)
            def _():
                pl.semaphore_signal(
                    barrier, inc=1, device_id=(2 * z + xbit, l), device_id_type=MESH
                )

    @pl.when(d == 0)
    def _():
        u0[:, :halo] = jnp.zeros((2, halo, rows + 2 * TILE, cols), jnp.float32)

    @pl.when(d == depth_size - 1)
    def _():
        u0[:, halo + layers :] = jnp.zeros((2, halo, rows + 2 * TILE, cols), jnp.float32)

    for edge, first in ((l == 0, 0), (l == lat_size - 1, TILE + rows)):

        @pl.when(edge)
        def _():
            def clear(x, carry):
                for f in range(2):
                    u0[f, x, pl.ds(first, TILE), :] = jnp.zeros((TILE, cols), jnp.float32)
                return carry

            lax.fori_loop(0, layers + 2 * halo, clear, 0)

    peers = sum(
        jnp.minimum(n, 1) for n in (d, depth_size - 1 - d, l, lat_size - 1 - l)
    )
    pl.semaphore_wait(barrier, peers + (VIEWS - 1 if swap else 0))

    lat_copies, edge_copies, mid_copies, corner_copies = [], [], [], []
    groups = GROUPS if layers % GROUPS == 0 else 1
    depth = layers // groups
    for g in range(groups):
        lat_copies.append([])
        for way in range(2):
            row_from, row_to = ((rows - TILE, 0), (0, TILE + rows))[way]
            for f in range(2):
                copy = pltpu.make_async_remote_copy(
                    src_ref=fields[f].at[pl.ds(g * depth, depth), pl.ds(row_from, TILE), :],
                    dst_ref=u0.at[f, pl.ds(halo + g * depth, depth), pl.ds(row_to, TILE), :],
                    send_sem=ys_sem.at[g, way, f],
                    recv_sem=yr_sem.at[g, way, f],
                    device_id=(d, (right, left)[way]),
                    device_id_type=MESH,
                )
                entry = ((has_high, has_low)[way], (has_low, has_high)[way], copy)
                lat_copies[g].append(entry)
    pieces = ((0, TILE), (rows - TILE, TILE), (TILE, rows - 2 * TILE))
    for piece, (row, size) in enumerate(pieces):
        for way in range(2):
            layer_from, layer_to = ((layers - halo, 0), (0, halo + layers))[way]
            for f in range(2):
                copy = pltpu.make_async_remote_copy(
                    src_ref=fields[f].at[pl.ds(layer_from, halo), pl.ds(row, size), :],
                    dst_ref=u0.at[f, pl.ds(layer_to, halo), pl.ds(TILE + row, size), :],
                    send_sem=xs_sem.at[piece, way, f],
                    recv_sem=xr_sem.at[piece, way, f],
                    device_id=((up, down)[way], l),
                    device_id_type=MESH,
                )
                entry = ((has_next, has_prev)[way], (has_prev, has_next)[way], copy)
                (mid_copies if piece == 2 else edge_copies).append(entry)
    for side in range(2):
        layer = (0, halo + layers)[side]
        filled = (has_prev, has_next)[side]
        for way in range(2):
            row_from, row_to = ((rows, 0), (TILE, TILE + rows))[way]
            copy = pltpu.make_async_remote_copy(
                src_ref=u0.at[:, pl.ds(layer, halo), pl.ds(row_from, TILE), :],
                dst_ref=u0.at[:, pl.ds(layer, halo), pl.ds(row_to, TILE), :],
                send_sem=cs_sem.at[side, way],
                recv_sem=cr_sem.at[side, way],
                device_id=(d, (right, left)[way]),
                device_id_type=MESH,
            )
            sends = jnp.logical_and(filled, (has_high, has_low)[way])
            receives = jnp.logical_and(filled, (has_low, has_high)[way])
            corner_copies.append((sends, receives, copy))

    def start(entries):
        for sends, _receives, copy in entries:
            pl.when(sends)(copy.start)

    def arrive(entries):
        for _sends, receives, copy in entries:
            pl.when(receives)(copy.wait_recv)

    def leave(entries):
        for sends, _receives, copy in entries:
            pl.when(sends)(copy.wait_send)

    start(edge_copies)
    start(lat_copies[0])
    start(mid_copies)
    for g in range(1, groups):
        start(lat_copies[g])
    for copy in local:
        copy.wait()

    chebyshev = thetas(SWEEPS)
    first_row = TILE - REACH
    span = rows + 2 * REACH
    chunk = next(n for n in (24, 16, 8) if span % n == 0)
    lane = lax.broadcasted_iota(jnp.int32, (chunk, cols), 1)
    row_id = lax.broadcasted_iota(jnp.int32, (chunk, cols), 0)
    low_mask = jnp.where(jnp.logical_or(row_id >= REACH, has_low), 1.0, 0.0)
    high_mask = jnp.where(jnp.logical_or(row_id < chunk - REACH, has_high), 1.0, 0.0)

    def sweep(k, before, after, x_lo, x_hi, edge):
        def body(xs, carry):
            for x in xs:
                factor = None
                if edge:
                    inside = jnp.logical_and(
                        jnp.logical_or(x >= halo, has_prev),
                        jnp.logical_or(x < halo + layers, has_next),
                    )
                    factor = jnp.where(inside, 1.0, 0.0)
                for r0 in range(first_row, first_row + span, chunk):
                    here = pl.ds(r0, chunk)
                    values = [before[f, x, here, :] for f in range(2)]
                    if k == 0:
                        p, t = values
                        reaction = p * (1.0 - p) * (p - 0.5 + COUPLE * t)
                        sources = [p + TIME_STEP * reaction, t + LATENT * TIME_STEP * reaction]
                    else:
                        sources = [src[f, x, here, :] for f in range(2)]
                    for f in range(2):
                        u = values[f]
                        around = before[f, x - 1, here, :] + before[f, x + 1, here, :]
                        around = around + (
                            before[f, x, pl.ds(r0 - 1, chunk), :]
                            + before[f, x, pl.ds(r0 + 1, chunk), :]
                        )
                        around = around + (
                            jnp.where(lane == 0, 0.0, pltpu.roll(u, 1, 1))
                            + jnp.where(lane == cols - 1, 0.0, pltpu.roll(u, cols - 1, 1))
                        )
                        theta = chebyshev[f, k]
                        new = (
                            float(1.0 - (1.0 + 6.0 * DIFFUSION[f]) / theta) * u
                            + float(1.0 / theta) * sources[f]
                            + float(DIFFUSION[f] / theta) * around
                        )
                        if r0 == first_row:
                            new = new * low_mask
                        if r0 + chunk == first_row + span:
                            new = new * high_mask
                        if edge:
                            new = new * factor
                        after[f, x, here, :] = new
                        if k == 0:
                            src[f, x, here, :] = sources[f]
            return carry

        blocked(x_lo, x_hi, 4, body, 0)

    stages = (u0, u1, u2, u3)
    total = layers + 2 * halo
    ready = halo + 1
    for g in range(groups):
        arrive(lat_copies[g])
        until = halo + (g + 1) * depth - 1
        sweep(0, u0, u1, ready, until, False)
        ready = until
    for k in range(1, SWEEPS):
        sweep(k, stages[k], stages[k + 1], halo + 1 + k, halo + layers - 1 - k, False)

    half = rows // 2
    count = count_ref[0, 0]
    lane1 = lax.broadcasted_iota(jnp.int32, (TILE, cols), 1)
    first_lane, last_lane = lane1 == 0, lane1 == cols - 1
    opacity = 4.0 / (layers * depth_size)
    starts = range(0, half, TILE)

    def render(v, r0, x_lo, x_hi, carry):
        sy = 1 if SHEAR_Y[v] > 0 else -1
        sz = 1 if SHEAR_Z[v] > 0 else -1
        edge_lane = last_lane if sz > 0 else first_lane

        def layer(x, whole, groups):
            xf = lax.convert_element_type(x, jnp.float32)
            fy = xf * (abs(SHEAR_Y[v]) / layers) - whole
            fz = xf * (abs(SHEAR_Z[v]) / layers)
            far_z = jnp.where(edge_lane, 0.0, fz)
            near_z = 1.0 - fz
            scale = jnp.where(x < count, -opacity, 0.0)
            result = []
            for row, (trans, red, green, blue) in zip(starts, groups):
                sampled = []
                for f in range(2):
                    first = TILE + r0 + row
                    near = u3[f, x + halo, pl.ds(first + sy * whole, TILE), :]
                    far = u3[f, x + halo, pl.ds(first + sy * (whole + 1), TILE), :]
                    b = near + fy * (far - near)
                    beside = pltpu.roll(b, cols - 1 if sz > 0 else 1, 1)
                    sampled.append(near_z * b + far_z * beside)
                after = trans * jnp.exp(scale * (sampled[0] * sampled[0]))
                weight = trans - after
                s = sampled[1]
                q = s * s
                d1 = q + 1.0
                a = q + (1.0 + CENTERS[2] * CENTERS[2])
                b = (2.0 * CENTERS[2]) * s
                d0, d2 = a + b, a - b
                result.append(
                    (
                        after,
                        red + weight * pl.reciprocal(d0, approx=True),
                        green + weight * pl.reciprocal(d1, approx=True),
                        blue + weight * pl.reciprocal(d2, approx=True),
                    )
                )
            return result

        groups = [tuple(c[r : r + TILE] for c in carry) for r in starts]
        for lo, hi, whole in segments(x_lo, x_hi, SHEAR_Y[v], layers):

            def body(xs, inner, whole=whole):
                for x in xs:
                    inner = layer(x, whole, inner)
                return inner

            groups = blocked(lo, hi, STEP, body, groups)
        return tuple(jnp.concatenate([g[c] for g in groups], axis=0) for c in range(4))

    zero = jnp.zeros((half, cols), jnp.float32)
    one = jnp.ones((half, cols), jnp.float32)

    start_carry = (one, zero, zero, zero)
    order = [0, VIEWS - 1] + list(range(1, VIEWS - 1))
    units = [(v, h) for v in order for h in range(2)]
    for place in range(EARLY):
        v, h = units[place]
        inner = render(v, h * half, halo, layers - halo, start_carry)
        for c in range(4):
            stash[place, c] = inner[c]

    arrive(edge_copies)
    start(corner_copies)
    arrive(mid_copies)
    arrive(corner_copies)
    for k in range(SWEEPS):
        sweep(k, stages[k], stages[k + 1], 1 + k, halo + 1 + k, True)
        sweep(k, stages[k], stages[k + 1], halo + layers - 1 - k, total - 1 - k, True)

    outs = [
        pltpu.make_async_copy(
            u3.at[f, pl.ds(halo, layers), pl.ds(TILE, rows), :],
            (phase_out, heat_out)[f],
            out_sem.at[f],
        )
        for f in range(2)
    ]
    for copy in outs:
        copy.start()

    def piece_of(place):
        v, h = units[place]
        if place < EARLY:
            trans, *colours = render(v, h * half, 0, halo, start_carry)
            inner = [stash[place, c] for c in range(4)]
            carry = (trans * inner[0],) + tuple(
                colours[c] + trans * inner[1 + c] for c in range(3)
            )
            carry = render(v, h * half, layers - halo, layers, carry)
        else:
            carry = render(v, h * half, 0, layers, start_carry)
        trans, red, green, blue = carry
        return [red, green, blue, trans]

    if not swap:
        for place, (v, h) in enumerate(units):
            part = piece_of(place)
            for c in range(4):
                picture_ref[c, h * half : (h + 1) * half, v * cols : (v + 1) * cols] = part[c]
    else:
        quarter = half // 2
        left_lanes = lax.broadcasted_iota(jnp.int32, (quarter, cols), 1) < cols // 2

        def pair_copy(v, h):
            return pltpu.make_async_remote_copy(
                src_ref=sent.at[v, h],
                dst_ref=xrecv.at[v, h],
                send_sem=ps_sem.at[v, h],
                recv_sem=pr_sem.at[v, h],
                device_id=(partner, l),
                device_id_type=MESH,
            )

        def group_copy(v, h, slot):
            return pltpu.make_async_remote_copy(
                src_ref=merged.at[v, h],
                dst_ref=zrecv.at[slot, h],
                send_sem=zs_sem.at[v, h],
                recv_sem=zr_sem.at[slot, h],
                device_id=(2 * v + xbit, l),
                device_id_type=MESH,
            )

        def send_pair(place):
            v, h = units[place]
            part = piece_of(place)
            for c in range(4):
                lo, hi = part[c][:quarter], part[c][quarter:]
                lower = jnp.where(left_lanes, lo, pltpu.roll(hi, cols // 2, 1))
                upper = jnp.where(left_lanes, pltpu.roll(lo, cols // 2, 1), hi)
                keep[v, h, c] = jnp.where(xbit == 0, lower, upper)
                sent[v, h, c] = jnp.where(xbit == 0, upper, lower)
            pair_copy(v, h).start()

        def send_group(place):
            v, h = units[place]
            pair_copy(v, h).wait_recv()
            mine = [keep[v, h, c] for c in range(4)]
            other = [xrecv[v, h, c] for c in range(4)]
            front = [jnp.where(xbit == 0, m, o) for m, o in zip(mine, other)]
            behind = [jnp.where(xbit == 0, o, m) for m, o in zip(mine, other)]
            result = over(front, behind)

            @pl.when(myz == v)
            def _():
                for c in range(4):
                    zrecv[v, h, c] = result[c]

            @pl.when(myz != v)
            def _():
                for c in range(4):
                    merged[v, h, c] = result[c]
                group_copy(v, h, myz).start()

        for place in range(len(units)):
            send_pair(place)
            if place >= 2:
                send_group(place - 2)
        send_group(len(units) - 2)
        send_group(len(units) - 1)

        for h in range(2):
            for s in range(VIEWS):
                pl.when(myz != s)(group_copy(s, h, s).wait_recv)
            result = [zrecv[VIEWS - 1, h, c] for c in range(4)]
            for s in range(VIEWS - 2, -1, -1):
                result = over([zrecv[s, h, c] for c in range(4)], result)
            for c in range(4):
                picture_ref[h, c] = result[c]
        for v, h in units:
            pair_copy(v, h).wait_send()
            pl.when(myz != v)(group_copy(v, h, myz).wait_send)

    for entries in lat_copies:
        leave(entries)
    leave(edge_copies)
    leave(mid_copies)
    leave(corner_copies)
    for copy in outs:
        copy.wait()


def deliver(phase_ref, heat_ref, packed_ref, phase_out, heat_out, picture_ref, held, into, out):
    layers = phase_ref.shape[0]
    size = layers // CHUNKS
    pairs = ((phase_ref, phase_out), (heat_ref, heat_out))
    arrivals, departures = [], []
    for f, (source, target) in enumerate(pairs):
        for n in range(CHUNKS):
            part = pl.ds(n * size, size)
            arrivals.append(
                pltpu.make_async_copy(source.at[part], held.at[f, part], into.at[f, n])
            )
            departures.append(
                pltpu.make_async_copy(held.at[f, part], target.at[part], out.at[f, n])
            )
    for copy in arrivals:
        copy.start()
    halves, channels, quarter, cols = packed_ref.shape
    for h in range(halves):
        for c in range(channels):
            part = packed_ref[h, c]
            first = 2 * h * quarter
            picture_ref[c, first : first + quarter, :] = part[:, : cols // 2]
            picture_ref[c, first + quarter : first + 2 * quarter, :] = pltpu.roll(
                part, cols // 2, 1
            )[:, : cols // 2]
    for arrival, departure in zip(arrivals, departures):
        arrival.wait()
        departure.start()
    for copy in departures:
        copy.wait()


def from_partner(shard, axis, apart):
    return lax.ppermute(shard, axis, [(i, i ^ 1 << apart) for i in range(lax.axis_size(axis))])


def over_blend(in_front, behind):
    return jnp.concatenate(
        [in_front[:3] + in_front[3:] * behind[:3], in_front[3:] * behind[3:]], axis=0
    )


def binary_swap(picture, depth_size):
    row_count, pixels = picture.shape[1:]
    bit_count = depth_size.bit_length() - 1
    block_width = pixels >> bit_count
    shaped = picture.reshape((4, row_count) + (2,) * bit_count + (block_width,))
    permuted = (0, 1) + tuple(range(bit_count + 1, 1, -1)) + (bit_count + 2,)
    picture = jnp.transpose(shaped, permuted).reshape(4, row_count, pixels)
    my_index = lax.axis_index("depth")
    for b in range(bit_count):
        half_width = picture.shape[2] // 2
        front_half = picture[:, :, :half_width]
        second = picture[:, :, half_width:]
        upper_bit = my_index >> b & 1 == 1
        kept_half = jnp.where(upper_bit, second, front_half)
        sent_half = jnp.where(upper_bit, front_half, second)
        partner = from_partner(sent_half, "depth", b)
        in_front = jnp.where(upper_bit, partner, kept_half)
        behind = jnp.where(upper_bit, kept_half, partner)
        picture = over_blend(in_front, behind)
    return picture


def per_device(phase, temper, iface_count):
    layers, rows, cols = phase.shape
    depth_size = lax.axis_size("depth")
    lat_size = lax.axis_size("lat")
    swap = depth_size == 2 * VIEWS
    packed = (2, 4, rows // 4, cols)
    piece = packed if swap else (4, rows, VIEWS * cols)
    grid = (2, layers + 2 * SWEEPS, rows + 2 * TILE, cols)
    tile = (VIEWS,) + packed
    dma = pltpu.SemaphoreType.DMA
    phase_next, heat_next, picture = pl.pallas_call(
        functools.partial(kernel, depth_size, lat_size, swap),
        out_shape=(
            jax.ShapeDtypeStruct(phase.shape, jnp.float32),
            jax.ShapeDtypeStruct(phase.shape, jnp.float32),
            jax.ShapeDtypeStruct(piece, jnp.float32),
        ),
        in_specs=[
            pl.BlockSpec(memory_space=pl.ANY),
            pl.BlockSpec(memory_space=pl.ANY),
            pl.BlockSpec(memory_space=pltpu.SMEM),
        ],
        out_specs=(
            pl.BlockSpec(memory_space=pl.ANY),
            pl.BlockSpec(memory_space=pl.ANY),
            pl.BlockSpec(memory_space=pltpu.VMEM),
        ),
        scratch_shapes=[pltpu.VMEM(grid, jnp.float32) for _ in range(5)]
        + [pltpu.VMEM((EARLY, 4, rows // 2, cols), jnp.float32)]
        + [pltpu.VMEM(tile, jnp.float32) for _ in range(5)]
        + [
            dma((2,)),
            dma((2,)),
            dma((3, 2, 2)),
            dma((3, 2, 2)),
            dma((GROUPS, 2, 2)),
            dma((GROUPS, 2, 2)),
            dma((2, 2)),
            dma((2, 2)),
            dma((VIEWS, 2)),
            dma((VIEWS, 2)),
            dma((VIEWS, 2)),
            dma((VIEWS, 2)),
        ],
        compiler_params=pltpu.CompilerParams(
            collective_id=0, has_side_effects=True, vmem_limit_bytes=60 * 1024 * 1024
        ),
    )(phase, temper, iface_count)
    if not swap:
        return phase_next, heat_next, binary_swap(picture, depth_size)
    return pl.pallas_call(
        deliver,
        out_shape=(
            jax.ShapeDtypeStruct(phase.shape, jnp.float32),
            jax.ShapeDtypeStruct(phase.shape, jnp.float32),
            jax.ShapeDtypeStruct((4, rows, cols // 2), jnp.float32),
        ),
        in_specs=[
            pl.BlockSpec(memory_space=pl.ANY),
            pl.BlockSpec(memory_space=pl.ANY),
            pl.BlockSpec(memory_space=pltpu.VMEM),
        ],
        out_specs=(
            pl.BlockSpec(memory_space=pl.ANY),
            pl.BlockSpec(memory_space=pl.ANY),
            pl.BlockSpec(memory_space=pltpu.VMEM),
        ),
        scratch_shapes=[
            pltpu.VMEM((2,) + phase.shape, jnp.float32),
            dma((2, CHUNKS)),
            dma((2, CHUNKS)),
        ],
        compiler_params=pltpu.CompilerParams(vmem_limit_bytes=60 * 1024 * 1024),
    )(phase_next, heat_next, picture)


def solution(mesh):
    return jax.shard_map(
        per_device,
        mesh=mesh,
        in_specs=(P("depth", "lat", None), P("depth", "lat", None), P("depth", "lat")),
        out_specs=(P("depth", "lat", None), P("depth", "lat", None), P(None, "lat", "depth")),
        check_vma=False,
    )
```
